256 devices in a mesh: row: 8 (over x, core), col: 32 (over z, y).
Axes of the slice: x: 4, y: 4, z: 8, core: 2. Of those that a mesh axis runs over, the one named last changes fastest.
Arguments:
- pixels: float32 [224, 128, 4096], P(None, 'row', 'col'), may hold values from -6 to 6
- library: float32 [224, 4096], P(None, 'col'), may hold values from -0.375 to 0.375
- block_ids: int32 [8, 32, 2], replicated, may hold values from 0 to 31, as said below
- counts: int32 [8, 32], replicated, may hold values from 1 to 2
Outputs:
- abundance: float32 [2, 128, 128, 4096], P(None, None, 'row', 'col')
- library_grad: float32 [4096, 224], P('col')
The draws below stay inside these ranges and needn't reach their ends.
Inputs may be any that keep to these rules, and one draw needn't show every extreme that they name: `block_ids`: the two slots of a tile name different blocks; every block is named by some tile.
All inputs are finite; a program needn't handle non-finite values.
Results may differ from the reference program's by a relative error of at most 0.00018.
Values sent between devices are 32-bit elements; how exact they have to be, the bound alone decides.
A program may use at most 64 MiB of HBM per device.

```python
import jax
import jax.numpy as jnp
from jax import lax

BANDS = 224
BLOCK = 128
BLOCKS = 32
ACTIVE = 2
ITERS = 3
TILE_H = 16
TILE_W = 128
LIBRARY = 4096
HEIGHT = 128
WIDTH = 4096
N_ROW = 8
N_COL = 32


def draw_block_ids(key, part):
    key = jax.random.fold_in(key, 11)
    key_shift, key_offset, key_order = jax.random.split(key, 3)
    tile_count = N_ROW * N_COL
    shift_value = jax.random.randint(key_shift, (), 0, BLOCKS)
    order = jax.random.permutation(key_order, tile_count)
    first = (order + shift_value) % BLOCKS
    offsets = jax.random.randint(key_offset, (tile_count,), 1, BLOCKS)
    second = (first + offsets) % BLOCKS
    return jnp.stack([first, second], axis=1).reshape(N_ROW, N_COL, 2).astype(jnp.int32)


def touch_ends(entries, own_key, low, high):
    spot = [jax.random.randint(jax.random.fold_in(own_key, axis), (), 0, length) for axis, length in enumerate(entries.shape)]
    longest = entries.shape.index(max(entries.shape))
    neighbour = spot[:longest] + [(spot[longest] + 1) % entries.shape[longest]] + spot[longest + 1:]
    return entries.at[tuple(spot)].set(low).at[tuple(neighbour)].set(high)


def steps_of(rng, dims, shards, low, high):
    level = 1.0
    for dim, shards_of in shards:
        heights = jax.random.uniform(jax.random.fold_in(jax.random.fold_in(rng, 6), dim), (shards_of,), jnp.float32, low / len(shards), high / len(shards))
        level = level * jnp.repeat(jnp.exp(heights), dims[dim] // shards_of).reshape((-1,) + (1,) * (len(dims) - 1 - dim))
    return level


def gaussian(key, dims, deviation, limit, shards=(), dtype=jnp.bfloat16):
    result = deviation * jax.random.normal(key, dims, jnp.float32)
    if shards:
        result = result * steps_of(key, dims, shards, -0.22, 0.18)
    return jnp.clip(result, -limit, limit).astype(dtype)


def setup_inputs(seed: int = 0) -> dict:
    key_of = jax.random.split(jax.random.key(seed), 5)
    return {
        "pixels": gaussian(key_of[0], (BANDS, HEIGHT, WIDTH), 1.0, 6.0, ((1, 8), (2, 32)), jnp.float32),
        "library": gaussian(key_of[1], (BANDS, LIBRARY), BANDS ** -0.5, 0.375, ((1, 32),), jnp.float32),
        "block_ids": draw_block_ids(jax.random.fold_in(key_of[4], 71), 0),
        "counts": touch_ends(jax.random.randint(key_of[3], (N_ROW, N_COL), 1, 3), jax.random.fold_in(key_of[3], 1), 1, 2).astype(jnp.int32),
    }


step_size = 0.2
penalty = 1.0
smoothing = 0.5
threshold = 0.05


def split_into_tiles(image):
    chans = image.shape[0]
    shaped = image.reshape(chans, N_ROW, TILE_H, N_COL, TILE_W).transpose(1, 3, 0, 2, 4)
    return shaped.reshape(N_ROW * N_COL, chans, TILE_H * TILE_W)


def to_image(tiles):
    chans = tiles.shape[1]
    shaped = tiles.reshape(N_ROW, N_COL, chans, TILE_H, TILE_W).transpose(2, 0, 3, 1, 4)
    return shaped.reshape(chans, HEIGHT, WIDTH)


def reference(pixels, library, block_ids, counts):
    highest_precision = lax.Precision.HIGHEST
    tile_count = N_ROW * N_COL
    width_total = ACTIVE * BLOCK
    tile_ids = block_ids.reshape(tile_count, ACTIVE).astype(jnp.int32)
    in_use = (jnp.arange(ACTIVE)[None, :] < counts.reshape(tile_count, 1)).astype(jnp.float32)
    lib_blocks = library.reshape(BANDS, BLOCKS, BLOCK).transpose(1, 0, 2)
    chosen = lib_blocks[tile_ids] * in_use[:, :, None, None]
    spectra_library = chosen.transpose(0, 2, 1, 3).reshape(tile_count, BANDS, width_total)
    observed_pixels = split_into_tiles(pixels)
    abundance = jnp.zeros((width_total, HEIGHT, WIDTH), jnp.float32)
    sparse_copy = jnp.zeros_like(abundance)
    scaled_dual = jnp.zeros_like(abundance)
    for iterate in range(ITERS):
        residual_error = jnp.einsum('fes,fsy->fey', spectra_library, split_into_tiles(abundance), precision=highest_precision) - observed_pixels
        gradient_field = jnp.einsum('odz,ods->ozs', spectra_library, residual_error, precision=highest_precision)
        padded = jnp.pad(abundance, ((0, 0), (1, 1), (1, 1)))
        beside = padded[:, 2:, 1:-1] + padded[:, :-2, 1:-1] + padded[:, 1:-1, 2:] + padded[:, 1:-1, :-2]
        laplace = 4.0 * abundance - beside
        abundance = abundance - step_size * (to_image(gradient_field) + penalty * (abundance - sparse_copy + scaled_dual) + smoothing * laplace)
        sparse_copy = jnp.maximum(abundance + scaled_dual - threshold, 0.0)
        scaled_dual = scaled_dual + abundance - sparse_copy
    tile_abundances = split_into_tiles(abundance)
    residual_error = jnp.einsum('fes,fsy->fey', spectra_library, tile_abundances, precision=highest_precision) - observed_pixels
    tile_abundances = tile_abundances.reshape(tile_count, ACTIVE, BLOCK, TILE_H * TILE_W)
    tile_gradients = jnp.einsum('ewvx,edx->ewvd', tile_abundances, residual_error, precision=highest_precision)
    tile_gradients = tile_gradients * in_use[:, :, None, None] / (TILE_H * TILE_W)
    summed = jnp.zeros((BLOCKS, BLOCK, BANDS), jnp.float32)
    summed = summed.at[tile_ids.reshape(-1)].add(tile_gradients.reshape(tile_count * ACTIVE, BLOCK, BANDS))
    return abundance.reshape(ACTIVE, BLOCK, HEIGHT, WIDTH), summed.reshape(BLOCKS * BLOCK, BANDS)
```

```python
import functools

import jax
import jax.numpy as jnp
from jax import lax
from jax.experimental import pallas as pl
from jax.experimental.pallas import tpu as pltpu
from jax.sharding import PartitionSpec as P

MESH = pl.DeviceIdType.MESH
BANDS = 224
BLOCK = 128
SLOTS = 2
WIDE = SLOTS * BLOCK
TILE_H = 16
TILE_W = 128
PIX = TILE_H * TILE_W
PART = 32
PARTS = BANDS // PART
ROWS = 8
PAIR = 2 * TILE_W
PAIRS = PIX // PAIR
STEP = 0.2
THRESHOLD = 0.05
F32 = jnp.float32
BF16 = jnp.bfloat16


def nn(a, b):
    return lax.dot_general(a, b, (((1,), (0,)), ((), ())), preferred_element_type=F32)


def nt(a, b):
    return lax.dot_general(a, b, (((1,), (1,)), ((), ())), preferred_element_type=F32)


def split(x):
    hi = x.astype(BF16)
    return hi, (x - hi.astype(F32)).astype(BF16)


def kernel(
    cols, pix_hbm, lib, ids, counts, abund_hbm, lgrad,
    pix, lhi, llo, gath, bsend, spec, a1, a2, a3, obuf, ones, tri,
    hs, hr, gsend, grecv, gacc, gall, outt,
    send_a, recv_a, send_b, recv_b, send_h, recv_h, send_g, recv_g,
    send_t, recv_t, send_c, recv_c, sem_pix, sem_out,
):
    r = lax.axis_index("row")
    c = lax.axis_index("col")
    mine = pl.ds(pl.multiple_of(r * PART, PART), PART)

    def far(src, dst, ssem, rsem, dev):
        return pltpu.make_async_remote_copy(
            src_ref=src, dst_ref=dst, send_sem=ssem, recv_sem=rsem,
            device_id=dev, device_id_type=MESH,
        )

    pix_in = pltpu.make_async_copy(pix_hbm, pix, sem_pix)
    pix_in.start()

    barrier = pltpu.get_barrier_semaphore()

    def greet_col(k, _):
        pl.semaphore_signal(barrier, inc=1, device_id=(r, lax.rem(c + k, cols)), device_id_type=MESH)
        return 0

    def greet_row(k, _):
        pl.semaphore_signal(barrier, inc=1, device_id=(lax.rem(r + k, ROWS), c), device_id_type=MESH)
        return 0

    lax.fori_loop(1, cols, greet_col, 0)
    lax.fori_loop(1, ROWS, greet_row, 0)
    pl.semaphore_wait(barrier, cols - 1 + ROWS - 1)

    def lib_copy(k):
        return far(lib.at[mine], gath.at[c], send_a.at[k], recv_a.at[k], (r, lax.rem(c + k, cols)))

    @pl.when(r < PARTS)
    def _():
        def go(k, _):
            lib_copy(k).start()
            return 0

        lax.fori_loop(1, cols, go, 0)
        gath[c] = lib[mine, :]

    lane = lax.broadcasted_iota(jnp.int32, (64, PIX), 1)
    which = lax.rem(lax.broadcasted_iota(jnp.int32, (64, PIX), 0), 32)
    spot = jnp.where(which < TILE_H, which * TILE_W, (which - TILE_H) * TILE_W + TILE_W - 1)
    ones[...] = jnp.where(lane == spot, 1.0, 0.0).astype(BF16)
    ti = lax.broadcasted_iota(jnp.int32, (PAIR, PAIR), 0)
    tj = lax.broadcasted_iota(jnp.int32, (PAIR, PAIR), 1)
    near = (jnp.abs(ti - tj) == 1) & (ti // TILE_W == tj // TILE_W)
    tri[...] = jnp.where(near, 1.0, 0.0).astype(BF16)

    @pl.when(r == 0)
    def _():
        for a in (a1, a2):
            a[:, :TILE_W] = jnp.zeros((WIDE, TILE_W), F32)

    @pl.when(r == ROWS - 1)
    def _():
        for a in (a1, a2):
            a[:, TILE_W + PIX:] = jnp.zeros((WIDE, TILE_W), F32)

    @pl.when(c == 0)
    def _():
        for i in range(2):
            hr[i, :TILE_H] = jnp.zeros((TILE_H, WIDE), F32)

    @pl.when(c == cols - 1)
    def _():
        for i in range(2):
            hr[i, TILE_H:] = jnp.zeros((TILE_H, WIDE), F32)

    pix_in.wait()
    for h in range(TILE_H):
        hi, lo = split(pix[pl.ds(h, BANDS, TILE_H), :])
        lhi[WIDE:, h * TILE_W:(h + 1) * TILE_W] = hi
        llo[WIDE:, h * TILE_W:(h + 1) * TILE_W] = lo

    def choose(row, s):
        use = jnp.where(counts[row, c] > s, 1.0, 0.0)
        return gath[ids[row, c, s]] * use

    def spec_copy(k):
        return far(bsend.at[k], spec.at[:, mine, :], send_b.at[k], recv_b.at[r], (lax.rem(r + k, ROWS), c))

    @pl.when(r < PARTS)
    def _():
        def got(k, _):
            lib_copy(k).wait_recv()
            return 0

        lax.fori_loop(1, cols, got, 0)
        for k in range(1, ROWS):
            for s in range(SLOTS):
                bsend[k, s] = choose(lax.rem(r + k, ROWS), s)
            spec_copy(k).start()
        for s in range(SLOTS):
            spec[s, mine, :] = choose(r, s)

    for p in range(PARTS):
        @pl.when(r != p)
        def _():
            far(bsend.at[0], spec.at[:, p * PART:(p + 1) * PART, :], send_b.at[0], recv_b.at[p], (r, c)).wait_recv()

    spectra = jnp.concatenate([spec[0], spec[1]], axis=1)
    spectra_t = spectra.T
    s_hi, s_lo = split(spectra)
    w_hi, w_lo = split(STEP * spectra_t)

    def lanes(j, pad=0):
        return pl.ds(pl.multiple_of(j * PAIR + pad, TILE_W), PAIR)

    def keep(j, value):
        hi, lo = split(value)
        lhi[:WIDE, lanes(j)] = hi
        llo[:WIDE, lanes(j)] = lo

    def row_copies(i, a):
        up = far(a.at[:, TILE_W:2 * TILE_W], a.at[:, TILE_W + PIX:], send_h.at[i, 2], recv_h.at[i, 3], (r - 1, c))
        down = far(a.at[:, PIX:TILE_W + PIX], a.at[:, :TILE_W], send_h.at[i, 3], recv_h.at[i, 2], (r + 1, c))
        return up, down

    def col_copies(i):
        left = far(hs.at[i, :TILE_H], hr.at[i, TILE_H:], send_h.at[i, 0], recv_h.at[i, 1], (r, c - 1))
        right = far(hs.at[i, TILE_H:], hr.at[i, :TILE_H], send_h.at[i, 1], recv_h.at[i, 0], (r, c + 1))
        return left, right

    def edges(i, a, what):
        up, down = row_copies(i, a)
        left, right = col_copies(i)

        @pl.when(c > 0)
        def _():
            if what == "start":
                left.start()
            elif what == "send":
                left.wait_send()
            else:
                right.wait_recv()

        @pl.when(c < cols - 1)
        def _():
            if what == "start":
                right.start()
            elif what == "send":
                right.wait_send()
            else:
                left.wait_recv()

        @pl.when(r > 0)
        def _():
            if what == "start":
                up.start()
            elif what == "send":
                up.wait_send()
            else:
                down.wait_recv()

        @pl.when(r < ROWS - 1)
        def _():
            if what == "start":
                down.start()
            elif what == "send":
                down.wait_send()
            else:
                up.wait_recv()

    def pack(i):
        picked = ones[:32, :]
        hs[i] = nt(picked, lhi[:WIDE, :]) + nt(picked, llo[:WIDE, :])

    def first(j, _):
        p_hi = lhi[WIDE:, lanes(j)]
        p_lo = llo[WIDE:, lanes(j)]
        value = nn(w_hi, p_hi) + nn(w_hi, p_lo) + nn(w_lo, p_hi)
        a1[:, lanes(j, TILE_W)] = value
        keep(j, value)
        return 0

    lax.fori_loop(0, PAIRS, first, 0)
    pack(0)
    edges(0, a1, "start")

    t_hi, t_lo = split(spectra_t)
    gram = nn(t_hi, s_hi) + nn(t_hi, s_lo) + nn(t_lo, s_hi)
    gi = lax.broadcasted_iota(jnp.int32, (WIDE, WIDE), 0)
    gj = lax.broadcasted_iota(jnp.int32, (WIDE, WIDE), 1)
    update = jnp.where(gi == gj, 0.4, 0.0) - STEP * gram
    u_hi, u_lo = split(update)

    def inner(j, now, excess):
        a_hi = lhi[:WIDE, lanes(j)]
        a_lo = llo[:WIDE, lanes(j)]
        value = nn(u_hi, a_hi) + nn(u_hi, a_lo) + nn(u_lo, a_hi)
        beside = nn(a_hi, tri[...]) + nn(a_lo, tri[...])
        value = value + a1[:, lanes(j, TILE_W)] + STEP * (jnp.abs(excess) - THRESHOLD)
        return value, beside

    def middle(j, now):
        above = now[:, lanes(j)]
        below = now[:, lanes(j, 2 * TILE_W)]
        return above, below

    def second(j, _):
        own = a1[:, lanes(j, TILE_W)]
        value, beside = inner(j, a1, own - THRESHOLD)
        a2[:, lanes(j, TILE_W)] = value + 0.1 * beside
        return 0

    def third(j, _):
        own = a2[:, lanes(j, TILE_W)]
        excess = own + jnp.minimum(a1[:, lanes(j, TILE_W)] - THRESHOLD, 0.0)
        value, beside = inner(j, a2, excess)
        a3[:, lanes(j)] = value + 0.1 * beside
        return 0

    def columns(i):
        hi, lo = split(hr[i])
        return jnp.concatenate([hi.astype(F32), lo.astype(F32)], axis=0).T.astype(BF16)

    lax.fori_loop(0, PAIRS, second, 0)
    edges(0, a1, "recv")
    side1 = columns(0)

    def second_end(j, _):
        above, below = middle(j, a1)
        value = a2[:, lanes(j, TILE_W)] + 0.1 * (nn(side1, ones[:, lanes(j)]) + above + below)
        a2[:, lanes(j, TILE_W)] = value
        keep(j, value)
        return 0

    lax.fori_loop(0, PAIRS, second_end, 0)
    pack(1)
    edges(1, a2, "start")
    lax.fori_loop(0, PAIRS, third, 0)
    edges(1, a2, "recv")
    side2 = columns(1)

    def third_end(j, _):
        above, below = middle(j, a2)
        value = a3[:, lanes(j)] + 0.1 * (nn(side2, ones[:, lanes(j)]) + above + below)
        a3[:, lanes(j)] = value
        keep(j, value)
        return 0

    lax.fori_loop(0, PAIRS, third_end, 0)
    for h in range(TILE_H):
        obuf[pl.ds(h, WIDE, TILE_H), :] = a3[:, h * TILE_W:(h + 1) * TILE_W]
    out = pltpu.make_async_copy(obuf, abund_hbm, sem_out)
    out.start()

    both = (
        nt(lhi[...], lhi[:WIDE, :]) + nt(lhi[...], llo[:WIDE, :]) + nt(llo[...], lhi[:WIDE, :])
    )
    c_hi, c_lo = split(both[:WIDE])
    grad = nn(s_hi, c_hi) + nn(s_hi, c_lo) + nn(s_lo, c_hi) - both[WIDE:]
    for s in range(SLOTS):
        use = jnp.where(counts[r, c] > s, 1.0 / PIX, 0.0)
        gsend[s] = grad[:, s * BLOCK:(s + 1) * BLOCK] * use

    def grad_copy(p):
        return far(
            gsend.at[:, p * PART:(p + 1) * PART, :], grecv.at[r], send_g.at[p], recv_g.at[r], (p, c)
        )

    for p in range(PARTS):
        @pl.when(r != p)
        def _():
            grad_copy(p).start()

        @pl.when(r == p)
        def _():
            grecv[r] = gsend[:, p * PART:(p + 1) * PART, :]

    def owner_copy(k):
        owner = lax.rem(c + k, cols)
        return far(gacc.at[owner], gall.at[k], send_t.at[k], recv_t.at[k], (r, owner))

    def part_copy(k):
        return far(outt.at[mine], outt.at[mine], send_c.at[k], recv_c.at[r], (lax.rem(r + k, ROWS), c))

    def collect(owner):
        total = jnp.zeros((PART, BLOCK), F32)
        for q in range(ROWS):
            for s in range(SLOTS):
                total = total + jnp.where(ids[q, c, s] == owner, 1.0, 0.0) * grecv[q, s]
        gacc[owner] = total

    @pl.when(r < PARTS)
    def _():
        for q in range(ROWS):
            @pl.when(r != q)
            def _():
                far(gsend.at[:, :PART, :], grecv.at[q], send_g.at[0], recv_g.at[q], (q, c)).wait_recv()

        def go(k, _):
            collect(lax.rem(c + k, cols))
            owner_copy(k).start()
            return 0

        lax.fori_loop(1, cols, go, 0)
        collect(c)

        def take(k, total):
            owner_copy(k).wait_recv()
            return total + gall[k]

        outt[mine, :] = lax.fori_loop(1, cols, take, gacc[c])
        for k in range(1, ROWS):
            part_copy(k).start()

    for p in range(PARTS):
        @pl.when(r != p)
        def _():
            block = outt.at[p * PART:(p + 1) * PART]
            far(block, block, send_c.at[0], recv_c.at[p], (r, c)).wait_recv()

    lgrad[...] = outt[...].T

    @pl.when(r < PARTS)
    def _():
        def left(k, _):
            lib_copy(k).wait_send()
            owner_copy(k).wait_send()
            return 0

        lax.fori_loop(1, cols, left, 0)
        for k in range(1, ROWS):
            spec_copy(k).wait_send()
            part_copy(k).wait_send()

    for p in range(PARTS):
        @pl.when(r != p)
        def _():
            grad_copy(p).wait_send()

    edges(0, a1, "send")
    edges(1, a2, "send")
    out.wait()


def local(cols, pixels, library, block_ids, counts):
    dma = pltpu.SemaphoreType.DMA
    abundance, grad = pl.pallas_call(
        functools.partial(kernel, cols),
        out_shape=(
            jax.ShapeDtypeStruct((WIDE * TILE_H, TILE_W), F32),
            jax.ShapeDtypeStruct((BLOCK, BANDS), F32),
        ),
        in_specs=[
            pl.BlockSpec(memory_space=pl.ANY),
            pl.BlockSpec(memory_space=pltpu.VMEM),
            pl.BlockSpec(memory_space=pltpu.SMEM),
            pl.BlockSpec(memory_space=pltpu.SMEM),
        ],
        out_specs=(
            pl.BlockSpec(memory_space=pl.ANY),
            pl.BlockSpec(memory_space=pltpu.VMEM),
        ),
        scratch_shapes=[
            pltpu.VMEM((BANDS * TILE_H, TILE_W), F32),
            pltpu.VMEM((WIDE + BANDS, PIX), BF16),
            pltpu.VMEM((WIDE + BANDS, PIX), BF16),
            pltpu.VMEM((cols, PART, BLOCK), F32),
            pltpu.VMEM((ROWS, SLOTS, PART, BLOCK), F32),
            pltpu.VMEM((SLOTS, BANDS, BLOCK), F32),
            pltpu.VMEM((WIDE, PIX + 2 * TILE_W), F32),
            pltpu.VMEM((WIDE, PIX + 2 * TILE_W), F32),
            pltpu.VMEM((WIDE, PIX), F32),
            pltpu.VMEM((WIDE * TILE_H, TILE_W), F32),
            pltpu.VMEM((64, PIX), BF16),
            pltpu.VMEM((PAIR, PAIR), BF16),
            pltpu.VMEM((2, 32, WIDE), F32),
            pltpu.VMEM((2, 32, WIDE), F32),
            pltpu.VMEM((SLOTS, BANDS, BLOCK), F32),
            pltpu.VMEM((ROWS, SLOTS, PART, BLOCK), F32),
            pltpu.VMEM((cols, PART, BLOCK), F32),
            pltpu.VMEM((cols, PART, BLOCK), F32),
            pltpu.VMEM((BANDS, BLOCK), F32),
            dma((cols,)), dma((cols,)),
            dma((ROWS,)), dma((ROWS,)),
            dma((2, 4)), dma((2, 4)),
            dma((ROWS,)), dma((ROWS,)),
            dma((cols,)), dma((cols,)),
            dma((ROWS,)), dma((ROWS,)),
            dma, dma,
        ],
        compiler_params=pltpu.CompilerParams(
            collective_id=0, has_side_effects=True, vmem_limit_bytes=48 * 1024 * 1024
        ),
    )(pixels.reshape(BANDS * TILE_H, TILE_W), library, block_ids, counts)
    return abundance.reshape(SLOTS, BLOCK, TILE_H, TILE_W), grad


def solution(mesh):
    placed = (P(None, "row", "col"), P(None, "col"), P(), P())
    return jax.shard_map(
        functools.partial(local, mesh.shape["col"]),
        mesh=mesh,
        in_specs=placed,
        out_specs=(P(None, None, "row", "col"), P("col", None)),
        check_vma=False,
    )
```

```python
import functools

import jax
import jax.numpy as jnp
from jax import lax
from jax.experimental import pallas as pl
from jax.experimental.pallas import tpu as pltpu
from jax.sharding import PartitionSpec as P

MESH = pl.DeviceIdType.MESH
BANDS = 224
BLOCK = 128
SLOTS = 2
WIDE = SLOTS * BLOCK
TILE_H = 16
TILE_W = 128
PIX = TILE_H * TILE_W
PART = 32
PARTS = BANDS // PART
ROWS = 8
YS = 4
PAIR = 2 * TILE_W
PAIRS = PIX // PAIR
STEP = 0.2
THRESHOLD = 0.05
F32 = jnp.float32
BF16 = jnp.bfloat16


def nn(a, b):
    return lax.dot_general(a, b, (((1,), (0,)), ((), ())), preferred_element_type=F32)


def nt(a, b):
    return lax.dot_general(a, b, (((1,), (1,)), ((), ())), preferred_element_type=F32)


def split(x):
    hi = x.astype(BF16)
    return hi, (x - hi.astype(F32)).astype(BF16)


def kernel(
    cols, pix_hbm, lib_hbm, ids_hbm, counts_hbm, abund, lgrad,
    pix, ids, counts, lhi, llo, gath, bsend, spec, a1, a2, a3, ones,
    hs, hr, gsend, grecv, gacc, gy, gzs, gz,
    send_z, recv_z, send_y, recv_y, send_b, recv_b, send_h, recv_h, send_g, recv_g,
    send_ty, recv_ty, send_tz, recv_tz, send_c, recv_c, sem_in,
):
    ny = YS
    nz = cols // ny
    r = lax.axis_index("row")
    c = lax.axis_index("col")
    z = c // ny
    y = lax.rem(c, ny)
    mine = pl.ds(pl.multiple_of(r * PART, PART), PART)
    near_first = sorted(range(1, nz), key=lambda d: (min(d, nz - d), d))

    def far(src, dst, ssem, rsem, dev):
        return pltpu.make_async_remote_copy(
            src_ref=src, dst_ref=dst, send_sem=ssem, recv_sem=rsem,
            device_id=dev, device_id_type=MESH,
        )

    def on_z(d):
        return (r, lax.rem(z + d, nz) * ny + y)

    def on_y(e):
        return (r, z * ny + lax.rem(y + e, ny))

    def on_row(k):
        return (lax.rem(r + k, ROWS), c)

    pix_in = pltpu.make_async_copy(pix_hbm, pix, sem_in.at[0])
    ids_in = pltpu.make_async_copy(ids_hbm, ids, sem_in.at[1])
    counts_in = pltpu.make_async_copy(counts_hbm, counts, sem_in.at[2])

    @pl.when(r < PARTS)
    def _():
        pltpu.make_async_copy(lib_hbm.at[mine], gath.at[y, 0], sem_in.at[3]).start()

    ids_in.start()
    counts_in.start()
    pix_in.start()

    barrier = pltpu.get_barrier_semaphore()

    def greet(dev):
        pl.semaphore_signal(barrier, inc=1, device_id=dev, device_id_type=MESH)

    for d in range(1, nz):
        greet(on_z(d))
    for e in range(1, ny):
        greet(on_y(e))
    for k in range(1, ROWS):
        greet(on_row(k))

    @pl.when(c > 0)
    def _():
        greet((r, c - 1))

    @pl.when(c < cols - 1)
    def _():
        greet((r, c + 1))

    beside_cols = (c > 0).astype(jnp.int32) + (c < cols - 1).astype(jnp.int32)
    pl.semaphore_wait(barrier, nz - 1 + ny - 1 + ROWS - 1 + beside_cols)

    def lib_z(d):
        return far(gath.at[y, 0], gath.at[y, d], send_z.at[d], recv_z.at[d], on_z(d))

    def lib_y(d, e):
        block = gath.at[y, d]
        return far(block, block, send_y.at[d, e], recv_y.at[d, e], on_y(e))

    @pl.when(r < PARTS)
    def _():
        pltpu.make_async_copy(lib_hbm.at[mine], gath.at[y, 0], sem_in.at[3]).wait()
        for d in near_first:
            lib_z(d).start()
        for e in range(1, ny):
            lib_y(0, e).start()

    lane = lax.broadcasted_iota(jnp.int32, (64, PIX), 1)
    which = lax.rem(lax.broadcasted_iota(jnp.int32, (64, PIX), 0), 32)
    spot = jnp.where(which < TILE_H, which * TILE_W, (which - TILE_H) * TILE_W + TILE_W - 1)
    ones[...] = jnp.where(lane == spot, 1.0, 0.0).astype(BF16)

    @pl.when(r == 0)
    def _():
        for a in (a1, a2):
            a[:, :TILE_W] = jnp.zeros((WIDE, TILE_W), F32)

    @pl.when(r == ROWS - 1)
    def _():
        for a in (a1, a2):
            a[:, TILE_W + PIX:] = jnp.zeros((WIDE, TILE_W), F32)

    @pl.when(c == 0)
    def _():
        for i in range(2):
            hr[i, :TILE_H] = jnp.zeros((TILE_H, WIDE), F32)

    @pl.when(c == cols - 1)
    def _():
        for i in range(2):
            hr[i, TILE_H:] = jnp.zeros((TILE_H, WIDE), F32)

    pix_in.wait()
    for h in range(TILE_H):
        hi, lo = split(pix[pl.ds(h, BANDS, TILE_H), :])
        lhi[WIDE:, h * TILE_W:(h + 1) * TILE_W] = hi
        llo[WIDE:, h * TILE_W:(h + 1) * TILE_W] = lo
    ids_in.wait()
    counts_in.wait()

    def choose(row, s):
        block = ids[row, s, c]
        use = jnp.where(counts[row, c] > s, 1.0, 0.0)
        return gath[lax.rem(block, ny), lax.rem(z - block // ny + nz, nz)] * use

    def spec_copy(k):
        return far(bsend.at[k], spec.at[:, mine, :], send_b.at[k], recv_b.at[r], on_row(k))

    @pl.when(r < PARTS)
    def _():
        for d in near_first:
            lib_z(d).wait_recv()
            for e in range(1, ny):
                lib_y(d, e).start()
        for d in [0] + near_first:
            for e in range(1, ny):
                lib_y(d, e).wait_recv()
        for k in range(1, ROWS):
            for s in range(SLOTS):
                bsend[k, s] = choose(lax.rem(r + k, ROWS), s)
            spec_copy(k).start()
        for s in range(SLOTS):
            spec[s, mine, :] = choose(r, s)

    for p in range(PARTS):
        @pl.when(r != p)
        def _():
            far(bsend.at[0], spec.at[:, p * PART:(p + 1) * PART, :], send_b.at[0], recv_b.at[p], (r, c)).wait_recv()

    spectra = jnp.concatenate([spec[0], spec[1]], axis=1)
    s_hi, s_lo = split(spectra)
    t_hi, t_lo = split(spectra.T)

    def lanes(j, pad=0):
        return slice(j * PAIR + pad, (j + 1) * PAIR + pad)

    def keep(j, value):
        hi, lo = split(value)
        lhi[:WIDE, lanes(j)] = hi
        llo[:WIDE, lanes(j)] = lo

    def row_copies(i, a):
        up = far(a.at[:, TILE_W:2 * TILE_W], a.at[:, TILE_W + PIX:], send_h.at[i, 2], recv_h.at[i, 3], (r - 1, c))
        down = far(a.at[:, PIX:TILE_W + PIX], a.at[:, :TILE_W], send_h.at[i, 3], recv_h.at[i, 2], (r + 1, c))
        return up, down

    def col_copies(i):
        left = far(hs.at[i, :TILE_H], hr.at[i, TILE_H:], send_h.at[i, 0], recv_h.at[i, 1], (r, c - 1))
        right = far(hs.at[i, TILE_H:], hr.at[i, :TILE_H], send_h.at[i, 1], recv_h.at[i, 0], (r, c + 1))
        return left, right

    def act(low, high, pos, count, what):
        @pl.when(pos > 0)
        def _():
            if what == "start":
                low.start()
            elif what == "send":
                low.wait_send()
            else:
                high.wait_recv()

        @pl.when(pos < count - 1)
        def _():
            if what == "start":
                high.start()
            elif what == "send":
                high.wait_send()
            else:
                low.wait_recv()

    def edge_rows(i, a, what):
        act(*row_copies(i, a), r, ROWS, what)

    def edge_cols(i, what):
        act(*col_copies(i), c, cols, what)

    def pack(i):
        picked = ones[:32, :]
        hs[i] = nt(picked, lhi[:WIDE, :]) + nt(picked, llo[:WIDE, :])

    ends_first = [0, PAIRS - 1] + list(range(1, PAIRS - 1))

    for j in ends_first:
        p_hi = lhi[WIDE:, lanes(j)]
        p_lo = llo[WIDE:, lanes(j)]
        value = STEP * (nn(t_hi, p_hi) + nn(t_hi, p_lo) + nn(t_lo, p_hi))
        a1[:, lanes(j, TILE_W)] = value
        keep(j, value)
        if j == PAIRS - 1:
            edge_rows(0, a1, "start")
    pack(0)
    edge_cols(0, "start")

    gram = nn(t_hi, s_hi) + nn(t_hi, s_lo) + nn(t_lo, s_hi)
    gi = lax.broadcasted_iota(jnp.int32, (WIDE, WIDE), 0)
    gj = lax.broadcasted_iota(jnp.int32, (WIDE, WIDE), 1)
    u_hi, u_lo = split(jnp.where(gi == gj, 0.4, 0.0) - STEP * gram)
    column = lax.broadcasted_iota(jnp.int32, (WIDE, TILE_W), 1)

    def beside(own):
        halves = []
        for q in range(2):
            x = own[:, q * TILE_W:(q + 1) * TILE_W]
            from_left = jnp.where(column == 0, 0.0, pltpu.roll(x, 1, 1))
            from_right = jnp.where(column == TILE_W - 1, 0.0, pltpu.roll(x, TILE_W - 1, 1))
            halves.append(from_left + from_right)
        return jnp.concatenate(halves, axis=1)

    def inner(j, own, excess):
        a_hi = lhi[:WIDE, lanes(j)]
        a_lo = llo[:WIDE, lanes(j)]
        value = nn(u_hi, a_hi) + nn(u_hi, a_lo) + nn(u_lo, a_hi)
        value = value + a1[:, lanes(j, TILE_W)] + STEP * (jnp.abs(excess) - THRESHOLD)
        return value + 0.1 * beside(own)

    def columns(i):
        hi, lo = split(hr[i])
        return jnp.concatenate([hi.astype(F32), lo.astype(F32)], axis=0).T.astype(BF16)

    def outer(j, side, a):
        return 0.1 * (nn(side, ones[:, lanes(j)]) + a[:, lanes(j)] + a[:, lanes(j, 2 * TILE_W)])

    for j in range(PAIRS):
        own = a1[:, lanes(j, TILE_W)]
        a2[:, lanes(j, TILE_W)] = inner(j, own, own - THRESHOLD)
    edge_rows(0, a1, "recv")
    edge_cols(0, "recv")
    side1 = columns(0)
    for j in ends_first:
        value = a2[:, lanes(j, TILE_W)] + outer(j, side1, a1)
        a2[:, lanes(j, TILE_W)] = value
        keep(j, value)
        if j == PAIRS - 1:
            edge_rows(1, a2, "start")
    pack(1)
    edge_cols(1, "start")
    for j in range(PAIRS):
        own = a2[:, lanes(j, TILE_W)]
        excess = own + jnp.minimum(a1[:, lanes(j, TILE_W)] - THRESHOLD, 0.0)
        a3[:, lanes(j)] = inner(j, own, excess)
    edge_rows(1, a2, "recv")
    edge_cols(1, "recv")
    side2 = columns(1)
    for j in range(PAIRS):
        value = a3[:, lanes(j)] + outer(j, side2, a2)
        a3[:, lanes(j)] = value
        keep(j, value)

    both = (
        nt(lhi[...], lhi[:WIDE, :]) + nt(lhi[...], llo[:WIDE, :]) + nt(llo[...], lhi[:WIDE, :])
    )
    c_hi, c_lo = split(both[:WIDE])
    grad = nn(s_hi, c_hi) + nn(s_hi, c_lo) + nn(s_lo, c_hi) - both[WIDE:]
    for s in range(SLOTS):
        use = jnp.where(counts[r, c] > s, 1.0 / PIX, 0.0)
        gsend[s] = grad[:, s * BLOCK:(s + 1) * BLOCK] * use

    def grad_copy(p):
        return far(
            gsend.at[:, p * PART:(p + 1) * PART, :], grecv.at[r], send_g.at[p], recv_g.at[r], (p, c)
        )

    for p in range(PARTS):
        @pl.when(r != p)
        def _():
            grad_copy(p).start()

        @pl.when(r == p)
        def _():
            grecv[r] = gsend[:, p * PART:(p + 1) * PART, :]

    for h in range(TILE_H):
        abund[pl.ds(h, WIDE, TILE_H), :] = a3[:, h * TILE_W:(h + 1) * TILE_W]

    def sum_y(d, e):
        return far(gacc.at[e, d], gy.at[e, d], send_ty.at[d, e], recv_ty.at[d, e], on_y(e))

    def sum_z(d):
        return far(gzs.at[d], gz.at[d], send_tz.at[d], recv_tz.at[d], on_z(d))

    def part_copy(k):
        return far(lgrad.at[mine], lgrad.at[mine], send_c.at[k], recv_c.at[r], on_row(k))

    far_first = near_first[::-1] + [0]

    @pl.when(r < PARTS)
    def _():
        for q in range(ROWS):
            @pl.when(r != q)
            def _():
                far(gsend.at[:, :PART, :], grecv.at[q], send_g.at[0], recv_g.at[q], (q, c)).wait_recv()

        named = [[ids[q, s, c] for s in range(SLOTS)] for q in range(ROWS)]
        for d in far_first:
            for e in list(range(1, ny)) + [0]:
                owner = lax.rem(z + d, nz) * ny + lax.rem(y + e, ny)
                total = jnp.zeros((PART, BLOCK), F32)
                for q in range(ROWS):
                    for s in range(SLOTS):
                        total = total + jnp.where(named[q][s] == owner, 1.0, 0.0) * grecv[q, s]
                gacc[e, d] = total
                if e:
                    sum_y(d, e).start()
        for d in far_first:
            total = gacc[0, d]
            for e in range(1, ny):
                sum_y(d, e).wait_recv()
                total = total + gy[e, d]
            if d:
                gzs[d] = total
                sum_z(d).start()
        for d in near_first[::-1]:
            sum_z(d).wait_recv()
            total = total + gz[d]
        lgrad[mine, :] = total
        for k in range(1, ROWS):
            part_copy(k).start()

    for p in range(PARTS):
        @pl.when(r != p)
        def _():
            block = lgrad.at[p * PART:(p + 1) * PART]
            far(block, block, send_c.at[0], recv_c.at[p], (r, c)).wait_recv()

    @pl.when(r < PARTS)
    def _():
        for d in range(nz):
            if d:
                lib_z(d).wait_send()
                sum_z(d).wait_send()
            for e in range(1, ny):
                lib_y(d, e).wait_send()
                sum_y(d, e).wait_send()
        for k in range(1, ROWS):
            spec_copy(k).wait_send()
            part_copy(k).wait_send()

    for p in range(PARTS):
        @pl.when(r != p)
        def _():
            grad_copy(p).wait_send()

    for i, a in enumerate((a1, a2)):
        edge_rows(i, a, "send")
        edge_cols(i, "send")


def local(cols, pixels, library, block_ids, counts):
    dma = pltpu.SemaphoreType.DMA
    ny = YS
    nz = cols // ny
    hbm = pl.BlockSpec(memory_space=pltpu.HBM)
    vmem = pl.BlockSpec(memory_space=pltpu.VMEM)
    abundance, grad = pl.pallas_call(
        functools.partial(kernel, cols),
        out_shape=(
            jax.ShapeDtypeStruct((WIDE * TILE_H, TILE_W), F32),
            jax.ShapeDtypeStruct((BANDS, BLOCK), F32),
        ),
        in_specs=[hbm] * 4,
        out_specs=(vmem, vmem),
        scratch_shapes=[
            pltpu.VMEM((BANDS * TILE_H, TILE_W), F32),
            pltpu.SMEM((ROWS, SLOTS, cols), jnp.int32),
            pltpu.SMEM((ROWS, cols), jnp.int32),
            pltpu.VMEM((WIDE + BANDS, PIX), BF16),
            pltpu.VMEM((WIDE + BANDS, PIX), BF16),
            pltpu.VMEM((ny, nz, PART, BLOCK), F32),
            pltpu.VMEM((ROWS, SLOTS, PART, BLOCK), F32),
            pltpu.VMEM((SLOTS, BANDS, BLOCK), F32),
            pltpu.VMEM((WIDE, PIX + 2 * TILE_W), F32),
            pltpu.VMEM((WIDE, PIX + 2 * TILE_W), F32),
            pltpu.VMEM((WIDE, PIX), F32),
            pltpu.VMEM((64, PIX), BF16),
            pltpu.VMEM((2, 32, WIDE), F32),
            pltpu.VMEM((2, 32, WIDE), F32),
            pltpu.VMEM((SLOTS, BANDS, BLOCK), F32),
            pltpu.VMEM((ROWS, SLOTS, PART, BLOCK), F32),
            pltpu.VMEM((ny, nz, PART, BLOCK), F32),
            pltpu.VMEM((ny, nz, PART, BLOCK), F32),
            pltpu.VMEM((nz, PART, BLOCK), F32),
            pltpu.VMEM((nz, PART, BLOCK), F32),
            dma((nz,)), dma((nz,)),
            dma((nz, ny)), dma((nz, ny)),
            dma((ROWS,)), dma((ROWS,)),
            dma((2, 4)), dma((2, 4)),
            dma((ROWS,)), dma((ROWS,)),
            dma((nz, ny)), dma((nz, ny)),
            dma((nz,)), dma((nz,)),
            dma((ROWS,)), dma((ROWS,)),
            dma((4,)),
        ],
        compiler_params=pltpu.CompilerParams(
            collective_id=0, has_side_effects=True, vmem_limit_bytes=48 * 1024 * 1024
        ),
    )(
        pixels.reshape(BANDS * TILE_H, TILE_W), library,
        block_ids.transpose(0, 2, 1), counts,
    )
    return abundance.reshape(SLOTS, BLOCK, TILE_H, TILE_W), grad.T


def solution(mesh):
    placed = (P(None, "row", "col"), P(None, "col"), P(), P())
    return jax.shard_map(
        functools.partial(local, mesh.shape["col"]),
        mesh=mesh,
        in_specs=placed,
        out_specs=(P(None, None, "row", "col"), P("col", None)),
        check_vma=False,
    )
```

```python
import functools

import jax
import jax.numpy as jnp
from jax import lax
from jax.experimental import pallas as pl
from jax.experimental.pallas import tpu as pltpu
from jax.sharding import PartitionSpec as P

MESH = pl.DeviceIdType.MESH
BANDS = 224
BLOCK = 128
SLOTS = 2
WIDE = SLOTS * BLOCK
TILE_H = 16
TILE_W = 128
PIX = TILE_H * TILE_W
PART = 32
SIZES = (32, 24)
CHIP = 56
ROWS = 8
COPIES = 8
VMEM_LIMIT = 60 * 1024 * 1024
YS = 4
PAIR = 2 * TILE_W
PAIRS = PIX // PAIR
STEP = 0.2
THRESHOLD = 0.05
F32 = jnp.float32
BF16 = jnp.bfloat16


def nn(a, b):
    return lax.dot_general(a, b, (((1,), (0,)), ((), ())), preferred_element_type=F32)


def nt(a, b):
    return lax.dot_general(a, b, (((1,), (1,)), ((), ())), preferred_element_type=F32)


def split(x):
    hi = x.astype(BF16)
    return hi, (x - hi.astype(F32)).astype(BF16)


def start_of(row):
    return row // 2 * CHIP + row % 2 * PART


def kernel(
    cols, pix_hbm, lib_hbm, ids_hbm, counts_hbm, abund_hbm, lgrad_hbm,
    pix, ids, counts, lhi, llo, gath, bsend, spec, a1, a2, a3, ones,
    rs, rr, hs, hr, gsend, grecv, gacc, gn, gy, gzs, gz, obuf, lgrad,
    send_z, recv_z, send_y, recv_y, send_b, recv_b, send_h, recv_h, send_g, recv_g,
    send_n, recv_n, send_ty, recv_ty, send_tz, recv_tz, send_c, recv_c, sem_in, sem_out,
):
    ny = YS
    nz = cols // ny
    r = lax.axis_index("row")
    c = lax.axis_index("col")
    z = c // ny
    y = lax.rem(c, ny)
    begin = pl.multiple_of(r // 2 * CHIP + lax.rem(r, 2) * PART, 8)

    def by_core(work):
        for k, size in enumerate(SIZES):
            pl.when(lax.rem(r, 2) == k)(functools.partial(work, size))

    def mine(size):
        return pl.ds(begin, size)

    near_first = sorted(range(1, nz), key=lambda d: (min(d, nz - d), d))

    def far(src, dst, ssem, rsem, dev):
        return pltpu.make_async_remote_copy(
            src_ref=src, dst_ref=dst, send_sem=ssem, recv_sem=rsem,
            device_id=dev, device_id_type=MESH,
        )

    def on_z(d):
        return (r, lax.rem(z + d, nz) * ny + y)

    def on_y(e):
        return (r, z * ny + lax.rem(y + e, ny))

    def on_row(k):
        return (lax.rem(r + k, ROWS), c)

    pix_in = pltpu.make_async_copy(pix_hbm, pix, sem_in.at[0])
    ids_in = pltpu.make_async_copy(ids_hbm, ids, sem_in.at[1])
    counts_in = pltpu.make_async_copy(counts_hbm, counts, sem_in.at[2])

    def lib_in(size):
        return pltpu.make_async_copy(
            lib_hbm.at[mine(size)], gath.at[y, 0, pl.ds(0, size)], sem_in.at[3]
        )

    by_core(lambda size: lib_in(size).start())
    ids_in.start()
    counts_in.start()
    pix_in.start()

    barrier = pltpu.get_barrier_semaphore()

    def greet(dev):
        pl.semaphore_signal(barrier, inc=1, device_id=dev, device_id_type=MESH)

    for d in range(1, nz):
        greet(on_z(d))
    for e in range(1, ny):
        greet(on_y(e))
    for k in range(1, ROWS):
        greet(on_row(k))

    @pl.when(c > 0)
    def _():
        greet((r, c - 1))

    @pl.when(c < cols - 1)
    def _():
        greet((r, c + 1))

    beside_cols = (c > 0).astype(jnp.int32) + (c < cols - 1).astype(jnp.int32)
    pl.semaphore_wait(barrier, nz - 1 + ny - 1 + ROWS - 1 + beside_cols)

    def lib_z(size, d):
        rows = pl.ds(0, size)
        return far(gath.at[y, 0, rows], gath.at[y, d, rows], send_z.at[d], recv_z.at[d], on_z(d))

    def lib_y(size, d, e):
        block = gath.at[y, d, pl.ds(0, size)]
        return far(block, block, send_y.at[d, e], recv_y.at[d, e], on_y(e))

    @by_core
    def _(size):
        lib_in(size).wait()
        for d in near_first:
            lib_z(size, d).start()
        for e in range(1, ny):
            lib_y(size, 0, e).start()

    lane = lax.broadcasted_iota(jnp.int32, (64, PIX), 1)
    which = lax.rem(lax.broadcasted_iota(jnp.int32, (64, PIX), 0), 32)
    spot = jnp.where(which < TILE_H, which * TILE_W, (which - TILE_H) * TILE_W + TILE_W - 1)
    ones[...] = jnp.where(lane == spot, 1.0, 0.0).astype(BF16)

    @pl.when(r == 0)
    def _():
        for i in range(2):
            rr[i, 0] = jnp.zeros((WIDE, TILE_W), F32)

    @pl.when(r == ROWS - 1)
    def _():
        for i in range(2):
            rr[i, 1] = jnp.zeros((WIDE, TILE_W), F32)

    @pl.when(c == 0)
    def _():
        for i in range(2):
            hr[i, :TILE_H] = jnp.zeros((TILE_H, WIDE), F32)

    @pl.when(c == cols - 1)
    def _():
        for i in range(2):
            hr[i, TILE_H:] = jnp.zeros((TILE_H, WIDE), F32)

    pix_in.wait()
    for h in range(TILE_H):
        hi, lo = split(pix[pl.ds(h, BANDS, TILE_H), :])
        lhi[WIDE:, h * TILE_W:(h + 1) * TILE_W] = hi
        llo[WIDE:, h * TILE_W:(h + 1) * TILE_W] = lo
    ids_in.wait()
    counts_in.wait()

    def choose(size, row, s):
        block = ids[row, s, c]
        use = jnp.where(counts[row, c] > s, 1.0, 0.0)
        return gath[lax.rem(block, ny), lax.rem(z - block // ny + nz, nz), :size] * use

    def spec_copy(size, k):
        return far(
            bsend.at[k, :, pl.ds(0, size)], spec.at[:, mine(size), :], send_b.at[k], recv_b.at[r], on_row(k)
        )

    @by_core
    def _(size):
        for d in near_first:
            lib_z(size, d).wait_recv()
            for e in range(1, ny):
                lib_y(size, d, e).start()
        for d in [0] + near_first:
            for e in range(1, ny):
                lib_y(size, d, e).wait_recv()
        for k in range(1, ROWS):
            for s in range(SLOTS):
                bsend[k, s, :size] = choose(size, lax.rem(r + k, ROWS), s)
            spec_copy(size, k).start()
        for s in range(SLOTS):
            spec[s, mine(size), :] = choose(size, r, s)

    for p in range(ROWS):
        @pl.when(r != p)
        def _():
            size = SIZES[p % 2]
            part = pl.ds(start_of(p), size)
            far(bsend.at[0, :, pl.ds(0, size)], spec.at[:, part, :], send_b.at[0], recv_b.at[p], (r, c)).wait_recv()

    spectra = jnp.concatenate([spec[0], spec[1]], axis=1)
    s_hi, s_lo = split(spectra)
    t_hi, t_lo = split(spectra.T)

    def lanes(j, pad=0):
        return slice(j * PAIR + pad, (j + 1) * PAIR + pad)

    def keep(j, value):
        hi, lo = split(value)
        lhi[:WIDE, lanes(j)] = hi
        llo[:WIDE, lanes(j)] = lo

    def row_copies(i):
        up = far(rs.at[i, 0], rr.at[i, 1], send_h.at[i, 2], recv_h.at[i, 3], (r - 1, c))
        down = far(rs.at[i, 1], rr.at[i, 0], send_h.at[i, 3], recv_h.at[i, 2], (r + 1, c))
        return up, down

    def col_copies(i):
        left = far(hs.at[i, :TILE_H], hr.at[i, TILE_H:], send_h.at[i, 0], recv_h.at[i, 1], (r, c - 1))
        right = far(hs.at[i, TILE_H:], hr.at[i, :TILE_H], send_h.at[i, 1], recv_h.at[i, 0], (r, c + 1))
        return left, right

    def act(low, high, pos, count, what):
        @pl.when(pos > 0)
        def _():
            if what == "start":
                low.start()
            elif what == "send":
                low.wait_send()
            else:
                high.wait_recv()

        @pl.when(pos < count - 1)
        def _():
            if what == "start":
                high.start()
            elif what == "send":
                high.wait_send()
            else:
                low.wait_recv()

    def edge_rows(i, what):
        act(*row_copies(i), r, ROWS, what)

    def edge_cols(i, what):
        act(*col_copies(i), c, cols, what)

    def pack(i):
        picked = ones[:32, :]
        hs[i] = nt(picked, lhi[:WIDE, :]) + nt(picked, llo[:WIDE, :])

    ends_first = [0, PAIRS - 1] + list(range(1, PAIRS - 1))

    for j in ends_first:
        p_hi = lhi[WIDE:, lanes(j)]
        p_lo = llo[WIDE:, lanes(j)]
        value = STEP * (nn(t_hi, p_hi) + nn(t_hi, p_lo) + nn(t_lo, p_hi))
        a1[:, lanes(j)] = value
        keep(j, value)
        if j == 0:
            rs[0, 0] = value[:, :TILE_W]
        if j == PAIRS - 1:
            rs[0, 1] = value[:, TILE_W:]
            edge_rows(0, "start")
    pack(0)
    edge_cols(0, "start")

    gram = nn(t_hi, s_hi) + nn(t_hi, s_lo) + nn(t_lo, s_hi)
    gi = lax.broadcasted_iota(jnp.int32, (WIDE, WIDE), 0)
    gj = lax.broadcasted_iota(jnp.int32, (WIDE, WIDE), 1)
    u_hi, u_lo = split(jnp.where(gi == gj, 0.4, 0.0) - STEP * gram)
    column = lax.broadcasted_iota(jnp.int32, (WIDE, TILE_W), 1)

    def beside(own):
        halves = []
        for q in range(2):
            x = own[:, q * TILE_W:(q + 1) * TILE_W]
            from_left = jnp.where(column == 0, 0.0, pltpu.roll(x, 1, 1))
            from_right = jnp.where(column == TILE_W - 1, 0.0, pltpu.roll(x, TILE_W - 1, 1))
            halves.append(from_left + from_right)
        return jnp.concatenate(halves, axis=1)

    def inner(j, own, excess):
        a_hi = lhi[:WIDE, lanes(j)]
        a_lo = llo[:WIDE, lanes(j)]
        value = nn(u_hi, a_hi) + nn(u_hi, a_lo) + nn(u_lo, a_hi)
        value = value + a1[:, lanes(j)] + STEP * (jnp.abs(excess) - THRESHOLD)
        return value + 0.1 * beside(own)

    def columns(i):
        hi, lo = split(hr[i])
        return jnp.concatenate([hi.astype(F32), lo.astype(F32)], axis=0).T.astype(BF16)

    def outer(i, j, side, a):
        if j == 0:
            above = jnp.concatenate([rr[i, 0], a[:, :TILE_W]], axis=1)
        else:
            above = a[:, lanes(j, -TILE_W)]
        if j == PAIRS - 1:
            below = jnp.concatenate([a[:, PIX - TILE_W:], rr[i, 1]], axis=1)
        else:
            below = a[:, lanes(j, TILE_W)]
        return 0.1 * (nn(side, ones[:, lanes(j)]) + above + below)

    for j in range(PAIRS):
        own = a1[:, lanes(j)]
        a2[:, lanes(j)] = inner(j, own, own - THRESHOLD)
    edge_rows(0, "recv")
    edge_cols(0, "recv")
    side1 = columns(0)
    for j in ends_first:
        value = a2[:, lanes(j)] + outer(0, j, side1, a1)
        a2[:, lanes(j)] = value
        keep(j, value)
        if j == 0:
            rs[1, 0] = value[:, :TILE_W]
        if j == PAIRS - 1:
            rs[1, 1] = value[:, TILE_W:]
            edge_rows(1, "start")
    pack(1)
    edge_cols(1, "start")
    for j in range(PAIRS):
        own = a2[:, lanes(j)]
        excess = own + jnp.minimum(a1[:, lanes(j)] - THRESHOLD, 0.0)
        a3[:, lanes(j)] = inner(j, own, excess)
    edge_rows(1, "recv")
    edge_cols(1, "recv")
    side2 = columns(1)
    for j in range(PAIRS):
        value = a3[:, lanes(j)] + outer(1, j, side2, a2)
        a3[:, lanes(j)] = value
        keep(j, value)

    both = (
        nt(lhi[...], lhi[:WIDE, :]) + nt(lhi[...], llo[:WIDE, :]) + nt(llo[...], lhi[:WIDE, :])
    )
    c_hi, c_lo = split(both[:WIDE])
    grad = nn(s_hi, c_hi) + nn(s_hi, c_lo) + nn(s_lo, c_hi) - both[WIDE:]
    for s in range(SLOTS):
        use = jnp.where(counts[r, c] > s, 1.0 / PIX, 0.0)
        gsend[s] = grad[:, s * BLOCK:(s + 1) * BLOCK] * use

    def grad_copy(p):
        size = SIZES[p % 2]
        return far(
            gsend.at[:, pl.ds(start_of(p), size), :], grecv.at[r, :, pl.ds(0, size)],
            send_g.at[p], recv_g.at[r], (p, c),
        )

    for p in range(ROWS):
        @pl.when(r != p)
        def _():
            grad_copy(p).start()

        @pl.when(r == p)
        def _():
            size = SIZES[p % 2]
            grecv[r, :, :size] = gsend[:, start_of(p):start_of(p) + size, :]

    for h in range(TILE_H):
        obuf[pl.ds(h, WIDE, TILE_H), :] = a3[:, h * TILE_W:(h + 1) * TILE_W]
    abund_out = pltpu.make_async_copy(obuf, abund_hbm, sem_out.at[0])
    abund_out.start()

    beside_z = [1, nz - 1] if nz > 3 else []
    far_first = [d for d in near_first[::-1] if d not in beside_z]

    def sum_n(size, i):
        rows = pl.ds(0, size)
        return far(
            gacc.at[:, beside_z[i], rows], gn.at[i, :, rows], send_n.at[i], recv_n.at[i], on_z(beside_z[i])
        )

    def sum_y(size, d, e):
        rows = pl.ds(0, size)
        return far(gacc.at[e, d, rows], gy.at[e, d, rows], send_ty.at[d, e], recv_ty.at[d, e], on_y(e))

    def sum_z(size, d):
        rows = pl.ds(0, size)
        return far(gzs.at[d, rows], gz.at[d, rows], send_tz.at[d], recv_tz.at[d], on_z(d))

    def part_copy(size, k):
        block = lgrad.at[mine(size)]
        return far(block, block, send_c.at[k], recv_c.at[r], on_row(k))

    @by_core
    def _(size):
        for q in range(ROWS):
            @pl.when(r != q)
            def _():
                far(
                    gsend.at[:, pl.ds(0, size), :], grecv.at[q, :, pl.ds(0, size)],
                    send_g.at[0], recv_g.at[q], (q, c),
                ).wait_recv()

        named = [[ids[q, s, c] for s in range(SLOTS)] for q in range(ROWS)]

        def collect(d, e):
            owner = lax.rem(z + d, nz) * ny + lax.rem(y + e, ny)
            total = jnp.zeros((size, BLOCK), F32)
            for q in range(ROWS):
                for s in range(SLOTS):
                    total = total + jnp.where(named[q][s] == owner, 1.0, 0.0) * grecv[q, s, :size]
            return total

        others = list(range(1, ny))
        for i, d in enumerate(beside_z):
            for e in range(ny):
                gacc[e, d, :size] = collect(d, e)
            sum_n(size, i).start()
        for d in far_first:
            for e in others + [0]:
                gacc[e, d, :size] = collect(d, e)
                if e:
                    sum_y(size, d, e).start()

        def forward(d):
            total = gacc[0, d, :size]
            for e in others:
                sum_y(size, d, e).wait_recv()
                total = total + gy[e, d, :size]
            if d:
                gzs[d, :size] = total
                sum_z(size, d).start()
            return total

        own = [collect(0, e) for e in range(ny)]
        for d in far_first[:1]:
            forward(d)
        for i in range(len(beside_z)):
            sum_n(size, i).wait_recv()
            own = [own[e] + gn[i, e, :size] for e in range(ny)]
        for e in others + [0]:
            gacc[e, 0, :size] = own[e]
            if e:
                sum_y(size, 0, e).start()
        for d in far_first[1:]:
            forward(d)
        total = forward(0)
        for d in far_first:
            sum_z(size, d).wait_recv()
            total = total + gz[d, :size]
        lgrad[mine(size), :] = total
        for k in range(1, ROWS):
            part_copy(size, k).start()

    for p in range(ROWS):
        @pl.when(r != p)
        def _():
            block = lgrad.at[pl.ds(start_of(p), SIZES[p % 2])]
            far(block, block, send_c.at[0], recv_c.at[p], (r, c)).wait_recv()

    lgrad_out = pltpu.make_async_copy(lgrad, lgrad_hbm, sem_out.at[1])
    lgrad_out.start()

    @by_core
    def _(size):
        for d in near_first:
            lib_z(size, d).wait_send()
        for d in range(nz):
            for e in range(1, ny):
                lib_y(size, d, e).wait_send()
        for i in range(len(beside_z)):
            sum_n(size, i).wait_send()
        for d in far_first:
            sum_z(size, d).wait_send()
        for d in far_first + [0]:
            for e in range(1, ny):
                sum_y(size, d, e).wait_send()
        for k in range(1, ROWS):
            spec_copy(size, k).wait_send()
            part_copy(size, k).wait_send()

    for p in range(ROWS):
        @pl.when(r != p)
        def _():
            grad_copy(p).wait_send()

    for i in range(2):
        edge_rows(i, "send")
        edge_cols(i, "send")
    abund_out.wait()
    lgrad_out.wait()


def finish(abund_in, lgrad_in, abund_out, lgrad_out, abund, lgrad, sems_in, sems_out):
    rows = abund_in.shape[0] // COPIES
    ways = [(lgrad_in, lgrad, lgrad_out)]
    for i in range(COPIES):
        part = pl.ds(i * rows, rows)
        ways.append((abund_in.at[part], abund.at[part], abund_out.at[part]))
    reads = [pltpu.make_async_copy(way[0], way[1], sems_in.at[i]) for i, way in enumerate(ways)]
    writes = [pltpu.make_async_copy(way[1], way[2], sems_out.at[i]) for i, way in enumerate(ways)]
    for read in reads:
        read.start()
    for read, write in zip(reads, writes):
        read.wait()
        write.start()
    for write in writes:
        write.wait()


def local(cols, pixels, library, block_ids, counts):
    dma = pltpu.SemaphoreType.DMA
    ny = YS
    nz = cols // ny
    hbm = pl.BlockSpec(memory_space=pltpu.HBM)
    shapes = (
        jax.ShapeDtypeStruct((WIDE * TILE_H, TILE_W), F32),
        jax.ShapeDtypeStruct((BANDS, BLOCK), F32),
    )
    abundance, grad = pl.pallas_call(
        functools.partial(kernel, cols),
        out_shape=shapes,
        in_specs=[hbm] * 4,
        out_specs=(hbm, hbm),
        scratch_shapes=[
            pltpu.VMEM((BANDS * TILE_H, TILE_W), F32),
            pltpu.SMEM((ROWS, SLOTS, cols), jnp.int32),
            pltpu.SMEM((ROWS, cols), jnp.int32),
            pltpu.VMEM((WIDE + BANDS, PIX), BF16),
            pltpu.VMEM((WIDE + BANDS, PIX), BF16),
            pltpu.VMEM((ny, nz, PART, BLOCK), F32),
            pltpu.VMEM((ROWS, SLOTS, PART, BLOCK), F32),
            pltpu.VMEM((SLOTS, BANDS, BLOCK), F32),
            pltpu.VMEM((WIDE, PIX), F32),
            pltpu.VMEM((WIDE, PIX), F32),
            pltpu.VMEM((WIDE, PIX), F32),
            pltpu.VMEM((64, PIX), BF16),
            pltpu.VMEM((2, 2, WIDE, TILE_W), F32),
            pltpu.VMEM((2, 2, WIDE, TILE_W), F32),
            pltpu.VMEM((2, 32, WIDE), F32),
            pltpu.VMEM((2, 32, WIDE), F32),
            pltpu.VMEM((SLOTS, BANDS, BLOCK), F32),
            pltpu.VMEM((ROWS, SLOTS, PART, BLOCK), F32),
            pltpu.VMEM((ny, nz, PART, BLOCK), F32),
            pltpu.VMEM((2, ny, PART, BLOCK), F32),
            pltpu.VMEM((ny, nz, PART, BLOCK), F32),
            pltpu.VMEM((nz, PART, BLOCK), F32),
            pltpu.VMEM((nz, PART, BLOCK), F32),
            pltpu.VMEM((WIDE * TILE_H, TILE_W), F32),
            pltpu.VMEM((BANDS, BLOCK), F32),
            dma((nz,)), dma((nz,)),
            dma((nz, ny)), dma((nz, ny)),
            dma((ROWS,)), dma((ROWS,)),
            dma((2, 4)), dma((2, 4)),
            dma((ROWS,)), dma((ROWS,)),
            dma((2,)), dma((2,)),
            dma((nz, ny)), dma((nz, ny)),
            dma((nz,)), dma((nz,)),
            dma((ROWS,)), dma((ROWS,)),
            dma((4,)), dma((2,)),
        ],
        compiler_params=pltpu.CompilerParams(
            collective_id=0, has_side_effects=True, vmem_limit_bytes=VMEM_LIMIT
        ),
    )(
        pixels.reshape(BANDS * TILE_H, TILE_W), library,
        block_ids.transpose(0, 2, 1), counts,
    )
    abundance, grad = pl.pallas_call(
        finish,
        out_shape=shapes,
        in_specs=[hbm, hbm],
        out_specs=(hbm, hbm),
        scratch_shapes=[
            pltpu.VMEM((WIDE * TILE_H, TILE_W), F32),
            pltpu.VMEM((BANDS, BLOCK), F32),
            dma((COPIES + 1,)), dma((COPIES + 1,)),
        ],
        compiler_params=pltpu.CompilerParams(vmem_limit_bytes=VMEM_LIMIT),
    )(abundance, grad)
    return abundance.reshape(SLOTS, BLOCK, TILE_H, TILE_W), grad.T


def solution(mesh):
    placed = (P(None, "row", "col"), P(None, "col"), P(), P())
    return jax.shard_map(
        functools.partial(local, mesh.shape["col"]),
        mesh=mesh,
        in_specs=placed,
        out_specs=(P(None, None, "row", "col"), P("col", None)),
        check_vma=False,
    )
```

```python
import functools

import jax
import jax.numpy as jnp
from jax import lax
from jax.experimental import pallas as pl
from jax.experimental.pallas import tpu as pltpu
from jax.sharding import PartitionSpec as P

MESH = pl.DeviceIdType.MESH
BANDS = 224
BLOCK = 128
SLOTS = 2
WIDE = SLOTS * BLOCK
TILE_H = 16
TILE_W = 128
PIX = TILE_H * TILE_W
PART = 32
SIZES = (32, 24)
CHIP = 56
ROWS = 8
COPIES = 8
VMEM_LIMIT = 60 * 1024 * 1024
YS = 4
PAIR = 2 * TILE_W
PAIRS = PIX // PAIR
STEP = 0.2
THRESHOLD = 0.05
F32 = jnp.float32
BF16 = jnp.bfloat16


def nn(a, b):
    return lax.dot_general(a, b, (((1,), (0,)), ((), ())), preferred_element_type=F32)


def nt(a, b):
    return lax.dot_general(a, b, (((1,), (1,)), ((), ())), preferred_element_type=F32)


def split(x):
    hi = x.astype(BF16)
    return hi, (x - hi.astype(F32)).astype(BF16)


def start_of(row):
    return row // 2 * CHIP + row % 2 * PART


def kernel(
    cols, pix_hbm, lib_hbm, ids_hbm, counts_hbm, abund_hbm, lgrad_hbm,
    pix, ids, counts, lhi, llo, gath, bsend, spec, a1, a2, a3, ones,
    rs, rr, hs, hr, cs, cr, gsend, grecv, gacc, gn, gy, gzs, gz, obuf, lgrad,
    send_z, recv_z, send_y, recv_y, send_b, recv_b, send_h, recv_h, send_k, recv_k, send_g, recv_g,
    send_n, recv_n, send_ty, recv_ty, send_tz, recv_tz, send_c, recv_c, sem_in, sem_out,
):
    ny = YS
    nz = cols // ny
    r = lax.axis_index("row")
    c = lax.axis_index("col")
    z = c // ny
    y = lax.rem(c, ny)
    begin = pl.multiple_of(r // 2 * CHIP + lax.rem(r, 2) * PART, 8)

    def by_core(work):
        for k, size in enumerate(SIZES):
            pl.when(lax.rem(r, 2) == k)(functools.partial(work, size))

    def mine(size):
        return pl.ds(begin, size)

    near_first = sorted(range(1, nz), key=lambda d: (min(d, nz - d), d))

    def far(src, dst, ssem, rsem, dev):
        return pltpu.make_async_remote_copy(
            src_ref=src, dst_ref=dst, send_sem=ssem, recv_sem=rsem,
            device_id=dev, device_id_type=MESH,
        )

    def on_z(d):
        return (r, lax.rem(z + d, nz) * ny + y)

    def on_y(e):
        return (r, z * ny + lax.rem(y + e, ny))

    def on_row(k):
        return (lax.rem(r + k, ROWS), c)

    pix_in = pltpu.make_async_copy(pix_hbm, pix, sem_in.at[0])
    ids_in = pltpu.make_async_copy(ids_hbm, ids, sem_in.at[1])
    counts_in = pltpu.make_async_copy(counts_hbm, counts, sem_in.at[2])

    def lib_in(size):
        return pltpu.make_async_copy(
            lib_hbm.at[mine(size)], gath.at[y, 0, pl.ds(0, size)], sem_in.at[3]
        )

    by_core(lambda size: lib_in(size).start())
    ids_in.start()
    counts_in.start()
    pix_in.start()

    barrier = pltpu.get_barrier_semaphore()

    def greet(dev):
        pl.semaphore_signal(barrier, inc=1, device_id=dev, device_id_type=MESH)

    for d in range(1, nz):
        greet(on_z(d))
    for e in range(1, ny):
        greet(on_y(e))
    for k in range(1, ROWS):
        greet(on_row(k))

    @pl.when(c > 0)
    def _():
        greet((r, c - 1))

    @pl.when(c < cols - 1)
    def _():
        greet((r, c + 1))

    corners = ((-1, -1, 0, 3), (1, -1, TILE_H - 1, 2), (-1, 1, TILE_H, 1), (1, 1, 2 * TILE_H - 1, 0))

    def within(dr, dc):
        return (r + dr >= 0) & (r + dr < ROWS) & (c + dc >= 0) & (c + dc < cols)

    across = jnp.int32(0)
    for dr, dc, _, _ in corners:
        across = across + within(dr, dc).astype(jnp.int32)

        @pl.when(within(dr, dc))
        def _():
            greet((r + dr, c + dc))

    beside_cols = (c > 0).astype(jnp.int32) + (c < cols - 1).astype(jnp.int32)
    pl.semaphore_wait(barrier, nz - 1 + ny - 1 + ROWS - 1 + beside_cols + across)

    def lib_z(size, d):
        rows = pl.ds(0, size)
        return far(gath.at[y, 0, rows], gath.at[y, d, rows], send_z.at[d], recv_z.at[d], on_z(d))

    def lib_y(size, d, e):
        block = gath.at[y, d, pl.ds(0, size)]
        return far(block, block, send_y.at[d, e], recv_y.at[d, e], on_y(e))

    @by_core
    def _(size):
        lib_in(size).wait()
        for d in near_first:
            lib_z(size, d).start()
        for e in range(1, ny):
            lib_y(size, 0, e).start()

    lane = lax.broadcasted_iota(jnp.int32, (64, PIX), 1)
    which = lax.rem(lax.broadcasted_iota(jnp.int32, (64, PIX), 0), 32)
    spot = jnp.where(which < TILE_H, which * TILE_W, (which - TILE_H) * TILE_W + TILE_W - 1)
    ones[...] = jnp.where(lane == spot, 1.0, 0.0).astype(BF16)

    @pl.when(r == 0)
    def _():
        for i in range(2):
            rr[i, 0] = jnp.zeros((WIDE, TILE_W), F32)

    @pl.when(r == ROWS - 1)
    def _():
        for i in range(2):
            rr[i, 1] = jnp.zeros((WIDE, TILE_W), F32)

    @pl.when(c == 0)
    def _():
        for i in range(2):
            hr[i, :TILE_H] = jnp.zeros((TILE_H, WIDE), F32)

    @pl.when(c == cols - 1)
    def _():
        for i in range(2):
            hr[i, TILE_H:] = jnp.zeros((TILE_H, WIDE), F32)

    for dr, dc, _, place in corners:
        @pl.when(jnp.logical_not(within(dr, dc)))
        def _():
            cr[3 - place] = jnp.zeros((8, WIDE), F32)

    pix_in.wait()
    for h in range(TILE_H):
        hi, lo = split(pix[pl.ds(h, BANDS, TILE_H), :])
        lhi[WIDE:, h * TILE_W:(h + 1) * TILE_W] = hi
        llo[WIDE:, h * TILE_W:(h + 1) * TILE_W] = lo
    ids_in.wait()
    counts_in.wait()

    def choose(size, row, s):
        block = ids[row, s, c]
        use = jnp.where(counts[row, c] > s, 1.0, 0.0)
        return gath[lax.rem(block, ny), lax.rem(z - block // ny + nz, nz), :size] * use

    def spec_copy(size, k):
        return far(
            bsend.at[k, :, pl.ds(0, size)], spec.at[:, mine(size), :], send_b.at[k], recv_b.at[r], on_row(k)
        )

    @by_core
    def _(size):
        for d in near_first:
            lib_z(size, d).wait_recv()
            for e in range(1, ny):
                lib_y(size, d, e).start()
        for d in [0] + near_first:
            for e in range(1, ny):
                lib_y(size, d, e).wait_recv()
        for k in range(1, ROWS):
            for s in range(SLOTS):
                bsend[k, s, :size] = choose(size, lax.rem(r + k, ROWS), s)
            spec_copy(size, k).start()
        for s in range(SLOTS):
            spec[s, mine(size), :] = choose(size, r, s)

    for p in range(ROWS):
        @pl.when(r != p)
        def _():
            size = SIZES[p % 2]
            part = pl.ds(start_of(p), size)
            far(bsend.at[0, :, pl.ds(0, size)], spec.at[:, part, :], send_b.at[0], recv_b.at[p], (r, c)).wait_recv()

    spectra = jnp.concatenate([spec[0], spec[1]], axis=1)
    s_hi, s_lo = split(spectra)
    t_hi, t_lo = split(spectra.T)

    def lanes(j, pad=0):
        return slice(j * PAIR + pad, (j + 1) * PAIR + pad)

    def keep(j, value):
        hi, lo = split(value)
        lhi[:WIDE, lanes(j)] = hi
        llo[:WIDE, lanes(j)] = lo

    def row_copies(i):
        up = far(rs.at[i, 0], rr.at[i, 1], send_h.at[i, 2], recv_h.at[i, 3], (r - 1, c))
        down = far(rs.at[i, 1], rr.at[i, 0], send_h.at[i, 3], recv_h.at[i, 2], (r + 1, c))
        return up, down

    def col_copies(i):
        left = far(hs.at[i, :TILE_H], hr.at[i, TILE_H:], send_h.at[i, 0], recv_h.at[i, 1], (r, c - 1))
        right = far(hs.at[i, TILE_H:], hr.at[i, :TILE_H], send_h.at[i, 1], recv_h.at[i, 0], (r, c + 1))
        return left, right

    def act(low, high, pos, count, what):
        @pl.when(pos > 0)
        def _():
            if what == "start":
                low.start()
            elif what == "send":
                low.wait_send()
            else:
                high.wait_recv()

        @pl.when(pos < count - 1)
        def _():
            if what == "start":
                high.start()
            elif what == "send":
                high.wait_send()
            else:
                low.wait_recv()

    def edge_rows(i, what):
        act(*row_copies(i), r, ROWS, what)

    def edge_cols(i, what):
        act(*col_copies(i), c, cols, what)

    def pack(i):
        picked = ones[:32, :]
        hs[i] = nt(picked, lhi[:WIDE, :]) + nt(picked, llo[:WIDE, :])

    ends_first = [0, PAIRS - 1] + list(range(1, PAIRS - 1))

    def corner_copy(i):
        dr, dc, _, place = corners[i]
        return far(cs.at[i], cr.at[place], send_k.at[i], recv_k.at[place], (r + dr, c + dc))

    def edge_corners(what):
        for i, (dr, dc, row, place) in enumerate(corners):
            @pl.when(within(dr, dc))
            def _():
                if what == "start":
                    cs[i] = jnp.broadcast_to(hs[0, row:row + 1, :], (8, WIDE))
                    corner_copy(i).start()
                elif what == "send":
                    corner_copy(i).wait_send()
                else:
                    corner_copy(3 - i).wait_recv()

    for j in ends_first:
        p_hi = lhi[WIDE:, lanes(j)]
        p_lo = llo[WIDE:, lanes(j)]
        value = STEP * (nn(t_hi, p_hi) + nn(t_hi, p_lo) + nn(t_lo, p_hi))
        a1[:, lanes(j)] = value
        keep(j, value)
        if j == 0:
            rs[0, 0] = value[:, :TILE_W]
        if j == PAIRS - 1:
            rs[0, 1] = value[:, TILE_W:]
            edge_rows(0, "start")
    pack(0)
    edge_cols(0, "start")
    edge_corners("start")

    gram = nn(t_hi, s_hi) + nn(t_hi, s_lo) + nn(t_lo, s_hi)
    gi = lax.broadcasted_iota(jnp.int32, (WIDE, WIDE), 0)
    gj = lax.broadcasted_iota(jnp.int32, (WIDE, WIDE), 1)
    u_hi, u_lo = split(jnp.where(gi == gj, 0.4, 0.0) - STEP * gram)
    column = lax.broadcasted_iota(jnp.int32, (WIDE, TILE_W), 1)

    def beside(own):
        halves = []
        for q in range(2):
            x = own[:, q * TILE_W:(q + 1) * TILE_W]
            from_left = jnp.where(column == 0, 0.0, pltpu.roll(x, 1, 1))
            from_right = jnp.where(column == TILE_W - 1, 0.0, pltpu.roll(x, TILE_W - 1, 1))
            halves.append(from_left + from_right)
        return jnp.concatenate(halves, axis=1)

    blank = jnp.zeros((WIDE, TILE_W), F32)

    def inner(j, a, excess):
        own = a[:, lanes(j)]
        a_hi = lhi[:WIDE, lanes(j)]
        a_lo = llo[:WIDE, lanes(j)]
        value = nn(u_hi, a_hi) + nn(u_hi, a_lo) + nn(u_lo, a_hi)
        value = value + a1[:, lanes(j)] + STEP * (jnp.abs(excess) - THRESHOLD)
        if j == 0:
            above = jnp.concatenate([blank, a[:, :TILE_W]], axis=1)
        else:
            above = a[:, lanes(j, -TILE_W)]
        if j == PAIRS - 1:
            below = jnp.concatenate([a[:, PIX - TILE_W:], blank], axis=1)
        else:
            below = a[:, lanes(j, TILE_W)]
        return value + 0.1 * (beside(own) + above + below)

    def columns(edge):
        hi, lo = split(edge)
        return jnp.concatenate([hi.astype(F32), lo.astype(F32)], axis=0).T.astype(BF16)

    def outer(j, side, above, below):
        value = nn(side, ones[:, lanes(j)])
        if j == 0:
            value = value + jnp.concatenate([above, blank], axis=1)
        if j == PAIRS - 1:
            value = value + jnp.concatenate([blank, below], axis=1)
        return 0.1 * value

    for j in ends_first:
        value = inner(j, a1, a1[:, lanes(j)] - THRESHOLD)
        a2[:, lanes(j)] = value
        keep(j, value)
        if j == 0:
            rs[1, 0] = value[:, :TILE_W]
        if j == PAIRS - 1:
            rs[1, 1] = value[:, TILE_W:]
            edge_rows(1, "start")
    pack(1)
    edge_cols(1, "start")
    edge_rows(0, "recv")
    edge_cols(0, "recv")
    side1 = columns(hr[0])
    for j in range(PAIRS):
        value = a2[:, lanes(j)] + outer(j, side1, rr[0, 0], rr[0, 1])
        a2[:, lanes(j)] = value
        keep(j, value)
    for j in range(PAIRS):
        excess = a2[:, lanes(j)] + jnp.minimum(a1[:, lanes(j)] - THRESHOLD, 0.0)
        a3[:, lanes(j)] = inner(j, a2, excess)
    edge_rows(1, "recv")
    edge_cols(1, "recv")
    edge_corners("recv")

    above2 = rr[1, 0] + jnp.where(r > 0, 0.1, 0.0) * a1[:, :TILE_W]
    below2 = rr[1, 1] + jnp.where(r < ROWS - 1, 0.1, 0.0) * a1[:, PIX - TILE_W:]
    row = lax.broadcasted_iota(jnp.int32, (2 * TILE_H, WIDE), 0)
    share = jnp.where(row < TILE_H, jnp.where(c > 0, 0.1, 0.0), jnp.where(c < cols - 1, 0.1, 0.0))
    edge2 = hr[1] + share * hs[0]
    for place, at in enumerate((0, TILE_H - 1, TILE_H, 2 * TILE_H - 1)):
        edge2 = edge2 + jnp.where(row == at, 0.2 * cr[place, :1, :], 0.0)
    side2 = columns(edge2)
    for j in range(PAIRS):
        value = a3[:, lanes(j)] + outer(j, side2, above2, below2)
        a3[:, lanes(j)] = value
        keep(j, value)

    both = (
        nt(lhi[...], lhi[:WIDE, :]) + nt(lhi[...], llo[:WIDE, :]) + nt(llo[...], lhi[:WIDE, :])
    )
    c_hi, c_lo = split(both[:WIDE])
    grad = nn(s_hi, c_hi) + nn(s_hi, c_lo) + nn(s_lo, c_hi) - both[WIDE:]
    for s in range(SLOTS):
        use = jnp.where(counts[r, c] > s, 1.0 / PIX, 0.0)
        gsend[s] = grad[:, s * BLOCK:(s + 1) * BLOCK] * use

    def grad_copy(p):
        size = SIZES[p % 2]
        return far(
            gsend.at[:, pl.ds(start_of(p), size), :], grecv.at[r, :, pl.ds(0, size)],
            send_g.at[p], recv_g.at[r], (p, c),
        )

    for p in range(ROWS):
        @pl.when(r != p)
        def _():
            grad_copy(p).start()

        @pl.when(r == p)
        def _():
            size = SIZES[p % 2]
            grecv[r, :, :size] = gsend[:, start_of(p):start_of(p) + size, :]

    for h in range(TILE_H):
        obuf[pl.ds(h, WIDE, TILE_H), :] = a3[:, h * TILE_W:(h + 1) * TILE_W]
    abund_out = pltpu.make_async_copy(obuf, abund_hbm, sem_out.at[0])
    abund_out.start()

    beside_z = [1, nz - 1] if nz > 3 else []
    far_first = [d for d in near_first[::-1] if d not in beside_z]

    def sum_n(size, i):
        rows = pl.ds(0, size)
        return far(
            gacc.at[:, beside_z[i], rows], gn.at[i, :, rows], send_n.at[i], recv_n.at[i], on_z(beside_z[i])
        )

    def sum_y(size, d, e):
        rows = pl.ds(0, size)
        return far(gacc.at[e, d, rows], gy.at[e, d, rows], send_ty.at[d, e], recv_ty.at[d, e], on_y(e))

    def sum_z(size, d):
        rows = pl.ds(0, size)
        return far(gzs.at[d, rows], gz.at[d, rows], send_tz.at[d], recv_tz.at[d], on_z(d))

    def part_copy(size, k):
        block = lgrad.at[mine(size)]
        return far(block, block, send_c.at[k], recv_c.at[r], on_row(k))

    @by_core
    def _(size):
        for q in range(ROWS):
            @pl.when(r != q)
            def _():
                far(
                    gsend.at[:, pl.ds(0, size), :], grecv.at[q, :, pl.ds(0, size)],
                    send_g.at[0], recv_g.at[q], (q, c),
                ).wait_recv()

        named = [[ids[q, s, c] for s in range(SLOTS)] for q in range(ROWS)]

        def collect(d, e):
            owner = lax.rem(z + d, nz) * ny + lax.rem(y + e, ny)
            total = jnp.zeros((size, BLOCK), F32)
            for q in range(ROWS):
                for s in range(SLOTS):
                    total = total + jnp.where(named[q][s] == owner, 1.0, 0.0) * grecv[q, s, :size]
            return total

        others = list(range(1, ny))
        for i, d in enumerate(beside_z):
            for e in range(ny):
                gacc[e, d, :size] = collect(d, e)
            sum_n(size, i).start()
        for d in far_first:
            for e in others + [0]:
                gacc[e, d, :size] = collect(d, e)
                if e:
                    sum_y(size, d, e).start()

        def forward(d):
            total = gacc[0, d, :size]
            for e in others:
                sum_y(size, d, e).wait_recv()
                total = total + gy[e, d, :size]
            if d:
                gzs[d, :size] = total
                sum_z(size, d).start()
            return total

        own = [collect(0, e) for e in range(ny)]
        for d in far_first[:1]:
            forward(d)
        for i in range(len(beside_z)):
            sum_n(size, i).wait_recv()
            own = [own[e] + gn[i, e, :size] for e in range(ny)]
        for e in others + [0]:
            gacc[e, 0, :size] = own[e]
            if e:
                sum_y(size, 0, e).start()
        for d in far_first[1:]:
            forward(d)
        total = forward(0)
        for d in far_first:
            sum_z(size, d).wait_recv()
            total = total + gz[d, :size]
        lgrad[mine(size), :] = total
        for k in range(1, ROWS):
            part_copy(size, k).start()

    for p in range(ROWS):
        @pl.when(r != p)
        def _():
            block = lgrad.at[pl.ds(start_of(p), SIZES[p % 2])]
            far(block, block, send_c.at[0], recv_c.at[p], (r, c)).wait_recv()

    lgrad_out = pltpu.make_async_copy(lgrad, lgrad_hbm, sem_out.at[1])
    lgrad_out.start()

    @by_core
    def _(size):
        for d in near_first:
            lib_z(size, d).wait_send()
        for d in range(nz):
            for e in range(1, ny):
                lib_y(size, d, e).wait_send()
        for i in range(len(beside_z)):
            sum_n(size, i).wait_send()
        for d in far_first:
            sum_z(size, d).wait_send()
        for d in far_first + [0]:
            for e in range(1, ny):
                sum_y(size, d, e).wait_send()
        for k in range(1, ROWS):
            spec_copy(size, k).wait_send()
            part_copy(size, k).wait_send()

    for p in range(ROWS):
        @pl.when(r != p)
        def _():
            grad_copy(p).wait_send()

    for i in range(2):
        edge_rows(i, "send")
        edge_cols(i, "send")
    edge_corners("send")
    abund_out.wait()
    lgrad_out.wait()


def finish(abund_in, lgrad_in, abund_out, lgrad_out, abund, lgrad, sems_in, sems_out):
    rows = abund_in.shape[0] // COPIES
    ways = [(lgrad_in, lgrad, lgrad_out)]
    for i in range(COPIES):
        part = pl.ds(i * rows, rows)
        ways.append((abund_in.at[part], abund.at[part], abund_out.at[part]))
    reads = [pltpu.make_async_copy(way[0], way[1], sems_in.at[i]) for i, way in enumerate(ways)]
    writes = [pltpu.make_async_copy(way[1], way[2], sems_out.at[i]) for i, way in enumerate(ways)]
    for read in reads:
        read.start()
    for read, write in zip(reads, writes):
        read.wait()
        write.start()
    for write in writes:
        write.wait()


def local(cols, pixels, library, block_ids, counts):
    dma = pltpu.SemaphoreType.DMA
    ny = YS
    nz = cols // ny
    hbm = pl.BlockSpec(memory_space=pltpu.HBM)
    shapes = (
        jax.ShapeDtypeStruct((WIDE * TILE_H, TILE_W), F32),
        jax.ShapeDtypeStruct((BANDS, BLOCK), F32),
    )
    abundance, grad = pl.pallas_call(
        functools.partial(kernel, cols),
        out_shape=shapes,
        in_specs=[hbm] * 4,
        out_specs=(hbm, hbm),
        scratch_shapes=[
            pltpu.VMEM((BANDS * TILE_H, TILE_W), F32),
            pltpu.SMEM((ROWS, SLOTS, cols), jnp.int32),
            pltpu.SMEM((ROWS, cols), jnp.int32),
            pltpu.VMEM((WIDE + BANDS, PIX), BF16),
            pltpu.VMEM((WIDE + BANDS, PIX), BF16),
            pltpu.VMEM((ny, nz, PART, BLOCK), F32),
            pltpu.VMEM((ROWS, SLOTS, PART, BLOCK), F32),
            pltpu.VMEM((SLOTS, BANDS, BLOCK), F32),
            pltpu.VMEM((WIDE, PIX), F32),
            pltpu.VMEM((WIDE, PIX), F32),
            pltpu.VMEM((WIDE, PIX), F32),
            pltpu.VMEM((64, PIX), BF16),
            pltpu.VMEM((2, 2, WIDE, TILE_W), F32),
            pltpu.VMEM((2, 2, WIDE, TILE_W), F32),
            pltpu.VMEM((2, 32, WIDE), F32),
            pltpu.VMEM((2, 32, WIDE), F32),
            pltpu.VMEM((4, 8, WIDE), F32),
            pltpu.VMEM((4, 8, WIDE), F32),
            pltpu.VMEM((SLOTS, BANDS, BLOCK), F32),
            pltpu.VMEM((ROWS, SLOTS, PART, BLOCK), F32),
            pltpu.VMEM((ny, nz, PART, BLOCK), F32),
            pltpu.VMEM((2, ny, PART, BLOCK), F32),
            pltpu.VMEM((ny, nz, PART, BLOCK), F32),
            pltpu.VMEM((nz, PART, BLOCK), F32),
            pltpu.VMEM((nz, PART, BLOCK), F32),
            pltpu.VMEM((WIDE * TILE_H, TILE_W), F32),
            pltpu.VMEM((BANDS, BLOCK), F32),
            dma((nz,)), dma((nz,)),
            dma((nz, ny)), dma((nz, ny)),
            dma((ROWS,)), dma((ROWS,)),
            dma((2, 4)), dma((2, 4)),
            dma((4,)), dma((4,)),
            dma((ROWS,)), dma((ROWS,)),
            dma((2,)), dma((2,)),
            dma((nz, ny)), dma((nz, ny)),
            dma((nz,)), dma((nz,)),
            dma((ROWS,)), dma((ROWS,)),
            dma((4,)), dma((2,)),
        ],
        compiler_params=pltpu.CompilerParams(
            collective_id=0, has_side_effects=True, vmem_limit_bytes=VMEM_LIMIT
        ),
    )(
        pixels.reshape(BANDS * TILE_H, TILE_W), library,
        block_ids.transpose(0, 2, 1), counts,
    )
    abundance, grad = pl.pallas_call(
        finish,
        out_shape=shapes,
        in_specs=[hbm, hbm],
        out_specs=(hbm, hbm),
        scratch_shapes=[
            pltpu.VMEM((WIDE * TILE_H, TILE_W), F32),
            pltpu.VMEM((BANDS, BLOCK), F32),
            dma((COPIES + 1,)), dma((COPIES + 1,)),
        ],
        compiler_params=pltpu.CompilerParams(vmem_limit_bytes=VMEM_LIMIT),
    )(abundance, grad)
    return abundance.reshape(SLOTS, BLOCK, TILE_H, TILE_W), grad.T


def solution(mesh):
    placed = (P(None, "row", "col"), P(None, "col"), P(), P())
    return jax.shard_map(
        functools.partial(local, mesh.shape["col"]),
        mesh=mesh,
        in_specs=placed,
        out_specs=(P(None, None, "row", "col"), P("col", None)),
        check_vma=False,
    )
```

```python
import functools

import jax
import jax.numpy as jnp
from jax import lax
from jax.experimental import pallas as pl
from jax.experimental.pallas import tpu as pltpu
from jax.sharding import PartitionSpec as P

MESH = pl.DeviceIdType.MESH
BANDS = 224
BLOCK = 128
SLOTS = 2
WIDE = SLOTS * BLOCK
TILE_H = 16
TILE_W = 128
PIX = TILE_H * TILE_W
PART = 32
SIZES = (32, 24)
CHIP = 56
ROWS = 8
COPIES = 4
ROW_ORDER = (4, 3, 5, 2, 6, 1, 7)
VMEM_LIMIT = 60 * 1024 * 1024
YS = 4
PAIR = 2 * TILE_W
PAIRS = PIX // PAIR
STEP = 0.2
THRESHOLD = 0.05
F32 = jnp.float32
BF16 = jnp.bfloat16


def nn(a, b):
    return lax.dot_general(a, b, (((1,), (0,)), ((), ())), preferred_element_type=F32)


def nt(a, b):
    return lax.dot_general(a, b, (((1,), (1,)), ((), ())), preferred_element_type=F32)


def split(x):
    hi = x.astype(BF16)
    return hi, (x - hi.astype(F32)).astype(BF16)


def start_of(row):
    return row // 2 * CHIP + row % 2 * PART


def kernel(
    cols, pix_hbm, lib_hbm, ids_hbm, counts_hbm, abund_hbm, lgrad_hbm,
    pix, ids, counts, lhi, llo, gath, bsend, spec, a1, a2, a3, ones,
    rs, rr, hs, hr, cs, cr, gsend, grecv, gacc, gn, gy, gzs, gz, obuf, lgrad,
    send_z, recv_z, send_y, recv_y, send_b, recv_b, send_h, recv_h, send_k, recv_k, send_g, recv_g,
    send_n, recv_n, send_ty, recv_ty, send_tz, recv_tz, send_c, recv_c, sem_in, sem_out,
):
    ny = YS
    nz = cols // ny
    r = lax.axis_index("row")
    c = lax.axis_index("col")
    z = c // ny
    y = lax.rem(c, ny)
    begin = pl.multiple_of(r // 2 * CHIP + lax.rem(r, 2) * PART, 8)

    def by_core(work):
        for k, size in enumerate(SIZES):
            pl.when(lax.rem(r, 2) == k)(functools.partial(work, size))

    def mine(size):
        return pl.ds(begin, size)

    near_first = sorted(range(1, nz), key=lambda d: (min(d, nz - d), d))

    def far(src, dst, ssem, rsem, dev):
        return pltpu.make_async_remote_copy(
            src_ref=src, dst_ref=dst, send_sem=ssem, recv_sem=rsem,
            device_id=dev, device_id_type=MESH,
        )

    def on_z(d):
        return (r, lax.rem(z + d, nz) * ny + y)

    def on_y(e):
        return (r, z * ny + lax.rem(y + e, ny))

    def on_row(k):
        return (lax.rem(r + k, ROWS), c)

    pix_in = pltpu.make_async_copy(pix_hbm, pix, sem_in.at[0])
    ids_in = pltpu.make_async_copy(ids_hbm, ids, sem_in.at[1])
    counts_in = pltpu.make_async_copy(counts_hbm, counts, sem_in.at[2])

    def lib_in(size):
        return pltpu.make_async_copy(
            lib_hbm.at[mine(size)], gath.at[y, 0, pl.ds(0, size)], sem_in.at[3]
        )

    by_core(lambda size: lib_in(size).start())
    ids_in.start()
    counts_in.start()
    pix_in.start()

    barrier = pltpu.get_barrier_semaphore()

    def greet(dev):
        pl.semaphore_signal(barrier, inc=1, device_id=dev, device_id_type=MESH)

    for d in near_first[::-1]:
        greet(on_z(d))
    for k in ROW_ORDER:
        greet(on_row(k))
    for e in range(1, ny):
        greet(on_y(e))

    @pl.when(c > 0)
    def _():
        greet((r, c - 1))

    @pl.when(c < cols - 1)
    def _():
        greet((r, c + 1))

    corners = ((-1, -1, 0, 3), (1, -1, TILE_H - 1, 2), (-1, 1, TILE_H, 1), (1, 1, 2 * TILE_H - 1, 0))

    def within(dr, dc):
        return (r + dr >= 0) & (r + dr < ROWS) & (c + dc >= 0) & (c + dc < cols)

    across = jnp.int32(0)
    for dr, dc, _, _ in corners:
        across = across + within(dr, dc).astype(jnp.int32)

        @pl.when(within(dr, dc))
        def _():
            greet((r + dr, c + dc))

    beside_cols = (c > 0).astype(jnp.int32) + (c < cols - 1).astype(jnp.int32)
    pl.semaphore_wait(barrier, nz - 1 + ny - 1 + ROWS - 1 + beside_cols + across)

    def lib_z(size, d):
        rows = pl.ds(0, size)
        return far(gath.at[y, 0, rows], gath.at[y, d, rows], send_z.at[d], recv_z.at[d], on_z(d))

    def lib_y(size, d, e):
        block = gath.at[y, d, pl.ds(0, size)]
        return far(block, block, send_y.at[d, e], recv_y.at[d, e], on_y(e))

    @by_core
    def _(size):
        lib_in(size).wait()
        for d in near_first:
            lib_z(size, d).start()
        for e in range(1, ny):
            lib_y(size, 0, e).start()

    lane = lax.broadcasted_iota(jnp.int32, (64, PIX), 1)
    which = lax.rem(lax.broadcasted_iota(jnp.int32, (64, PIX), 0), 32)
    spot = jnp.where(which < TILE_H, which * TILE_W, (which - TILE_H) * TILE_W + TILE_W - 1)
    ones[...] = jnp.where(lane == spot, 1.0, 0.0).astype(BF16)

    @pl.when(r == 0)
    def _():
        for i in range(2):
            rr[i, 0] = jnp.zeros((WIDE, TILE_W), F32)

    @pl.when(r == ROWS - 1)
    def _():
        for i in range(2):
            rr[i, 1] = jnp.zeros((WIDE, TILE_W), F32)

    @pl.when(c == 0)
    def _():
        for i in range(2):
            hr[i, :TILE_H] = jnp.zeros((TILE_H, WIDE), F32)

    @pl.when(c == cols - 1)
    def _():
        for i in range(2):
            hr[i, TILE_H:] = jnp.zeros((TILE_H, WIDE), F32)

    for dr, dc, _, place in corners:
        @pl.when(jnp.logical_not(within(dr, dc)))
        def _():
            cr[3 - place] = jnp.zeros((8, WIDE), F32)

    pix_in.wait()
    for h in range(TILE_H):
        hi, lo = split(pix[pl.ds(h, BANDS, TILE_H), :])
        lhi[WIDE:, h * TILE_W:(h + 1) * TILE_W] = hi
        llo[WIDE:, h * TILE_W:(h + 1) * TILE_W] = lo
    ids_in.wait()
    counts_in.wait()

    def choose(size, row, s):
        block = ids[row, s, c]
        use = jnp.where(counts[row, c] > s, 1.0, 0.0)
        return gath[lax.rem(block, ny), lax.rem(z - block // ny + nz, nz), :size] * use

    def spec_copy(size, k):
        return far(
            bsend.at[k, :, pl.ds(0, size)], spec.at[:, mine(size), :], send_b.at[k], recv_b.at[r], on_row(k)
        )

    @by_core
    def _(size):
        for d in near_first:
            lib_z(size, d).wait_recv()
            for e in range(1, ny):
                lib_y(size, d, e).start()
        for d in [0] + near_first:
            for e in range(1, ny):
                lib_y(size, d, e).wait_recv()
        for k in ROW_ORDER:
            for s in range(SLOTS):
                bsend[k, s, :size] = choose(size, lax.rem(r + k, ROWS), s)
            spec_copy(size, k).start()
        for s in range(SLOTS):
            spec[s, mine(size), :] = choose(size, r, s)

    for p in range(ROWS):
        @pl.when(r != p)
        def _():
            size = SIZES[p % 2]
            part = pl.ds(start_of(p), size)
            far(bsend.at[0, :, pl.ds(0, size)], spec.at[:, part, :], send_b.at[0], recv_b.at[p], (r, c)).wait_recv()

    spectra = jnp.concatenate([spec[0], spec[1]], axis=1)
    s_hi, s_lo = split(spectra)
    t_hi, t_lo = split(spectra.T)

    def lanes(j, pad=0):
        return slice(j * PAIR + pad, (j + 1) * PAIR + pad)

    def keep(j, value):
        hi, lo = split(value)
        lhi[:WIDE, lanes(j)] = hi
        llo[:WIDE, lanes(j)] = lo

    def row_copies(i):
        up = far(rs.at[i, 0], rr.at[i, 1], send_h.at[i, 2], recv_h.at[i, 3], (r - 1, c))
        down = far(rs.at[i, 1], rr.at[i, 0], send_h.at[i, 3], recv_h.at[i, 2], (r + 1, c))
        return up, down

    def col_copies(i):
        left = far(hs.at[i, :TILE_H], hr.at[i, TILE_H:], send_h.at[i, 0], recv_h.at[i, 1], (r, c - 1))
        right = far(hs.at[i, TILE_H:], hr.at[i, :TILE_H], send_h.at[i, 1], recv_h.at[i, 0], (r, c + 1))
        return left, right

    def act(low, high, pos, count, what):
        @pl.when(pos > 0)
        def _():
            if what == "start":
                low.start()
            elif what == "send":
                low.wait_send()
            else:
                high.wait_recv()

        @pl.when(pos < count - 1)
        def _():
            if what == "start":
                high.start()
            elif what == "send":
                high.wait_send()
            else:
                low.wait_recv()

    def edge_rows(i, what):
        act(*row_copies(i), r, ROWS, what)

    def edge_cols(i, what):
        act(*col_copies(i), c, cols, what)

    def pack(i):
        picked = ones[:32, :]
        hs[i] = nt(picked, lhi[:WIDE, :]) + nt(picked, llo[:WIDE, :])

    ends_first = [0, PAIRS - 1] + list(range(1, PAIRS - 1))

    def corner_copy(i):
        dr, dc, _, place = corners[i]
        return far(cs.at[i], cr.at[place], send_k.at[i], recv_k.at[place], (r + dr, c + dc))

    def edge_corners(what):
        for i, (dr, dc, row, place) in enumerate(corners):
            @pl.when(within(dr, dc))
            def _():
                if what == "start":
                    cs[i] = jnp.broadcast_to(hs[0, row:row + 1, :], (8, WIDE))
                    corner_copy(i).start()
                elif what == "send":
                    corner_copy(i).wait_send()
                else:
                    corner_copy(3 - i).wait_recv()

    for j in ends_first:
        p_hi = lhi[WIDE:, lanes(j)]
        p_lo = llo[WIDE:, lanes(j)]
        value = STEP * (nn(t_hi, p_hi) + nn(t_hi, p_lo) + nn(t_lo, p_hi))
        a1[:, lanes(j)] = value
        keep(j, value)
        if j == 0:
            rs[0, 0] = value[:, :TILE_W]
        if j == PAIRS - 1:
            rs[0, 1] = value[:, TILE_W:]
            edge_rows(0, "start")
    pack(0)
    edge_cols(0, "start")
    edge_corners("start")

    gram = nn(t_hi, s_hi) + nn(t_hi, s_lo) + nn(t_lo, s_hi)
    gi = lax.broadcasted_iota(jnp.int32, (WIDE, WIDE), 0)
    gj = lax.broadcasted_iota(jnp.int32, (WIDE, WIDE), 1)
    u_hi, u_lo = split(jnp.where(gi == gj, 0.4, 0.0) - STEP * gram)
    column = lax.broadcasted_iota(jnp.int32, (WIDE, TILE_W), 1)

    def beside(own):
        halves = []
        for q in range(2):
            x = own[:, q * TILE_W:(q + 1) * TILE_W]
            from_left = jnp.where(column == 0, 0.0, pltpu.roll(x, 1, 1))
            from_right = jnp.where(column == TILE_W - 1, 0.0, pltpu.roll(x, TILE_W - 1, 1))
            halves.append(from_left + from_right)
        return jnp.concatenate(halves, axis=1)

    blank = jnp.zeros((WIDE, TILE_W), F32)

    def inner(j, a, excess):
        own = a[:, lanes(j)]
        a_hi = lhi[:WIDE, lanes(j)]
        a_lo = llo[:WIDE, lanes(j)]
        value = nn(u_hi, a_hi) + nn(u_hi, a_lo) + nn(u_lo, a_hi)
        value = value + a1[:, lanes(j)] + STEP * (jnp.abs(excess) - THRESHOLD)
        if j == 0:
            above = jnp.concatenate([blank, a[:, :TILE_W]], axis=1)
        else:
            above = a[:, lanes(j, -TILE_W)]
        if j == PAIRS - 1:
            below = jnp.concatenate([a[:, PIX - TILE_W:], blank], axis=1)
        else:
            below = a[:, lanes(j, TILE_W)]
        return value + 0.1 * (beside(own) + above + below)

    def columns(edge):
        hi, lo = split(edge)
        return jnp.concatenate([hi.astype(F32), lo.astype(F32)], axis=0).T.astype(BF16)

    def outer(j, side, above, below):
        value = nn(side, ones[:, lanes(j)])
        if j == 0:
            value = value + jnp.concatenate([above, blank], axis=1)
        if j == PAIRS - 1:
            value = value + jnp.concatenate([blank, below], axis=1)
        return 0.1 * value

    for j in ends_first:
        value = inner(j, a1, a1[:, lanes(j)] - THRESHOLD)
        a2[:, lanes(j)] = value
        keep(j, value)
        if j == 0:
            rs[1, 0] = value[:, :TILE_W]
        if j == PAIRS - 1:
            rs[1, 1] = value[:, TILE_W:]
            edge_rows(1, "start")
    pack(1)
    edge_cols(1, "start")
    edge_rows(0, "recv")
    edge_cols(0, "recv")
    side1 = columns(hr[0])
    for j in range(PAIRS):
        value = a2[:, lanes(j)] + outer(j, side1, rr[0, 0], rr[0, 1])
        a2[:, lanes(j)] = value
        keep(j, value)
    for j in range(PAIRS):
        excess = a2[:, lanes(j)] + jnp.minimum(a1[:, lanes(j)] - THRESHOLD, 0.0)
        a3[:, lanes(j)] = inner(j, a2, excess)
    edge_rows(1, "recv")
    edge_cols(1, "recv")
    edge_corners("recv")

    above2 = rr[1, 0] + jnp.where(r > 0, 0.1, 0.0) * a1[:, :TILE_W]
    below2 = rr[1, 1] + jnp.where(r < ROWS - 1, 0.1, 0.0) * a1[:, PIX - TILE_W:]
    row = lax.broadcasted_iota(jnp.int32, (2 * TILE_H, WIDE), 0)
    share = jnp.where(row < TILE_H, jnp.where(c > 0, 0.1, 0.0), jnp.where(c < cols - 1, 0.1, 0.0))
    edge2 = hr[1] + share * hs[0]
    for place, at in enumerate((0, TILE_H - 1, TILE_H, 2 * TILE_H - 1)):
        edge2 = edge2 + jnp.where(row == at, 0.2 * cr[place, :1, :], 0.0)
    side2 = columns(edge2)
    for j in range(PAIRS):
        value = a3[:, lanes(j)] + outer(j, side2, above2, below2)
        a3[:, lanes(j)] = value
        keep(j, value)

    both = (
        nt(lhi[...], lhi[:WIDE, :]) + nt(lhi[...], llo[:WIDE, :]) + nt(llo[...], lhi[:WIDE, :])
    )
    c_hi, c_lo = split(both[:WIDE])
    grad = nn(s_hi, c_hi) + nn(s_hi, c_lo) + nn(s_lo, c_hi) - both[WIDE:]
    for s in range(SLOTS):
        use = jnp.where(counts[r, c] > s, 1.0 / PIX, 0.0)
        gsend[s] = grad[:, s * BLOCK:(s + 1) * BLOCK] * use

    def grad_copy(size, k):
        other = SIZES[(SIZES.index(size) + k) % 2]
        row, _ = on_row(k)
        first = pl.multiple_of(row // 2 * CHIP + lax.rem(row, 2) * PART, 8)
        return far(
            gsend.at[:, pl.ds(first, other), :], grecv.at[r, :, pl.ds(0, other)],
            send_g.at[k], recv_g.at[r], on_row(k),
        )

    @by_core
    def _(size):
        for k in ROW_ORDER:
            grad_copy(size, k).start()
        grecv[r, :, :size] = gsend[:, mine(size), :]

    for h in range(TILE_H):
        obuf[pl.ds(h, WIDE, TILE_H), :] = a3[:, h * TILE_W:(h + 1) * TILE_W]
    abund_out = pltpu.make_async_copy(obuf, abund_hbm, sem_out.at[0])
    abund_out.start()

    beside_z = [1, nz - 1] if nz > 3 else []
    far_first = [d for d in near_first[::-1] if d not in beside_z]

    def sum_n(size, i):
        rows = pl.ds(0, size)
        return far(
            gacc.at[:, beside_z[i], rows], gn.at[i, :, rows], send_n.at[i], recv_n.at[i], on_z(beside_z[i])
        )

    def sum_y(size, d, e):
        rows = pl.ds(0, size)
        return far(gacc.at[e, d, rows], gy.at[e, d, rows], send_ty.at[d, e], recv_ty.at[d, e], on_y(e))

    def sum_z(size, d):
        rows = pl.ds(0, size)
        return far(gzs.at[d, rows], gz.at[d, rows], send_tz.at[d], recv_tz.at[d], on_z(d))

    def part_copy(size, k):
        return far(
            lgrad.at[mine(size)], lgrad_hbm.at[mine(size)], send_c.at[k], recv_c.at[r], on_row(k)
        )

    def part_out(size):
        return pltpu.make_async_copy(lgrad.at[mine(size)], lgrad_hbm.at[mine(size)], sem_out.at[1])

    @by_core
    def _(size):
        for q in range(ROWS):
            @pl.when(r != q)
            def _():
                far(
                    gsend.at[:, pl.ds(0, size), :], grecv.at[q, :, pl.ds(0, size)],
                    send_g.at[0], recv_g.at[q], (q, c),
                ).wait_recv()

        named = [[ids[q, s, c] for s in range(SLOTS)] for q in range(ROWS)]

        def collect(d, e):
            owner = lax.rem(z + d, nz) * ny + lax.rem(y + e, ny)
            total = jnp.zeros((size, BLOCK), F32)
            for q in range(ROWS):
                for s in range(SLOTS):
                    total = total + jnp.where(named[q][s] == owner, 1.0, 0.0) * grecv[q, s, :size]
            return total

        others = list(range(1, ny))
        for i, d in enumerate(beside_z):
            for e in range(ny):
                gacc[e, d, :size] = collect(d, e)
            sum_n(size, i).start()
        for d in far_first:
            for e in others + [0]:
                gacc[e, d, :size] = collect(d, e)
                if e:
                    sum_y(size, d, e).start()

        def forward(d):
            total = gacc[0, d, :size]
            for e in others:
                sum_y(size, d, e).wait_recv()
                total = total + gy[e, d, :size]
            if d:
                gzs[d, :size] = total
                sum_z(size, d).start()
            return total

        own = [collect(0, e) for e in range(ny)]
        for d in far_first[:1]:
            forward(d)
        for i in range(len(beside_z)):
            sum_n(size, i).wait_recv()
            own = [own[e] + gn[i, e, :size] for e in range(ny)]
        for e in others + [0]:
            gacc[e, 0, :size] = own[e]
            if e:
                sum_y(size, 0, e).start()
        for d in far_first[1:]:
            forward(d)
        total = forward(0)
        for d in far_first:
            sum_z(size, d).wait_recv()
            total = total + gz[d, :size]
        lgrad[mine(size), :] = total
        for k in ROW_ORDER:
            part_copy(size, k).start()
        part_out(size).start()

        for d in near_first:
            lib_z(size, d).wait_send()
        for d in range(nz):
            for e in range(1, ny):
                lib_y(size, d, e).wait_send()
        for i in range(len(beside_z)):
            sum_n(size, i).wait_send()
        for d in far_first:
            sum_z(size, d).wait_send()
        for d in far_first + [0]:
            for e in range(1, ny):
                sum_y(size, d, e).wait_send()
        for k in ROW_ORDER:
            spec_copy(size, k).wait_send()
            grad_copy(size, k).wait_send()

    for i in range(2):
        edge_rows(i, "send")
        edge_cols(i, "send")
    edge_corners("send")
    abund_out.wait()

    for p in range(ROWS):
        @pl.when(r != p)
        def _():
            part = pl.ds(start_of(p), SIZES[p % 2])
            far(lgrad.at[part], lgrad_hbm.at[part], send_c.at[0], recv_c.at[p], (r, c)).wait_recv()

    @by_core
    def _(size):
        part_out(size).wait()
        for k in ROW_ORDER:
            part_copy(size, k).wait_send()


def finish(abund_in, lgrad_in, abund_out, lgrad_out, abund, lgrad, sems_in, sems_out):
    rows = abund_in.shape[0] // COPIES
    ways = [(lgrad_in, lgrad, lgrad_out)]
    for i in range(COPIES):
        part = pl.ds(i * rows, rows)
        ways.append((abund_in.at[part], abund.at[part], abund_out.at[part]))
    reads = [pltpu.make_async_copy(way[0], way[1], sems_in.at[i]) for i, way in enumerate(ways)]
    writes = [pltpu.make_async_copy(way[1], way[2], sems_out.at[i]) for i, way in enumerate(ways)]
    for read in reads:
        read.start()
    for read, write in zip(reads, writes):
        read.wait()
        write.start()
    for write in writes:
        write.wait()


def local(cols, pixels, library, block_ids, counts):
    dma = pltpu.SemaphoreType.DMA
    ny = YS
    nz = cols // ny
    hbm = pl.BlockSpec(memory_space=pltpu.HBM)
    shapes = (
        jax.ShapeDtypeStruct((WIDE * TILE_H, TILE_W), F32),
        jax.ShapeDtypeStruct((BANDS, BLOCK), F32),
    )
    abundance, grad = pl.pallas_call(
        functools.partial(kernel, cols),
        out_shape=shapes,
        in_specs=[hbm] * 4,
        out_specs=(hbm, hbm),
        scratch_shapes=[
            pltpu.VMEM((BANDS * TILE_H, TILE_W), F32),
            pltpu.SMEM((ROWS, SLOTS, cols), jnp.int32),
            pltpu.SMEM((ROWS, cols), jnp.int32),
            pltpu.VMEM((WIDE + BANDS, PIX), BF16),
            pltpu.VMEM((WIDE + BANDS, PIX), BF16),
            pltpu.VMEM((ny, nz, PART, BLOCK), F32),
            pltpu.VMEM((ROWS, SLOTS, PART, BLOCK), F32),
            pltpu.VMEM((SLOTS, BANDS, BLOCK), F32),
            pltpu.VMEM((WIDE, PIX), F32),
            pltpu.VMEM((WIDE, PIX), F32),
            pltpu.VMEM((WIDE, PIX), F32),
            pltpu.VMEM((64, PIX), BF16),
            pltpu.VMEM((2, 2, WIDE, TILE_W), F32),
            pltpu.VMEM((2, 2, WIDE, TILE_W), F32),
            pltpu.VMEM((2, 32, WIDE), F32),
            pltpu.VMEM((2, 32, WIDE), F32),
            pltpu.VMEM((4, 8, WIDE), F32),
            pltpu.VMEM((4, 8, WIDE), F32),
            pltpu.VMEM((SLOTS, BANDS, BLOCK), F32),
            pltpu.VMEM((ROWS, SLOTS, PART, BLOCK), F32),
            pltpu.VMEM((ny, nz, PART, BLOCK), F32),
            pltpu.VMEM((2, ny, PART, BLOCK), F32),
            pltpu.VMEM((ny, nz, PART, BLOCK), F32),
            pltpu.VMEM((nz, PART, BLOCK), F32),
            pltpu.VMEM((nz, PART, BLOCK), F32),
            pltpu.VMEM((WIDE * TILE_H, TILE_W), F32),
            pltpu.VMEM((BANDS, BLOCK), F32),
            dma((nz,)), dma((nz,)),
            dma((nz, ny)), dma((nz, ny)),
            dma((ROWS,)), dma((ROWS,)),
            dma((2, 4)), dma((2, 4)),
            dma((4,)), dma((4,)),
            dma((ROWS,)), dma((ROWS,)),
            dma((2,)), dma((2,)),
            dma((nz, ny)), dma((nz, ny)),
            dma((nz,)), dma((nz,)),
            dma((ROWS,)), dma((ROWS,)),
            dma((4,)), dma((2,)),
        ],
        compiler_params=pltpu.CompilerParams(
            collective_id=0, has_side_effects=True, vmem_limit_bytes=VMEM_LIMIT
        ),
    )(
        pixels.reshape(BANDS * TILE_H, TILE_W), library,
        block_ids.transpose(0, 2, 1), counts,
    )
    abundance, grad = pl.pallas_call(
        finish,
        out_shape=shapes,
        in_specs=[hbm, hbm],
        out_specs=(hbm, hbm),
        scratch_shapes=[
            pltpu.VMEM((WIDE * TILE_H, TILE_W), F32),
            pltpu.VMEM((BANDS, BLOCK), F32),
            dma((COPIES + 1,)), dma((COPIES + 1,)),
        ],
        compiler_params=pltpu.CompilerParams(vmem_limit_bytes=VMEM_LIMIT),
    )(abundance, grad)
    return abundance.reshape(SLOTS, BLOCK, TILE_H, TILE_W), grad.T


def solution(mesh):
    placed = (P(None, "row", "col"), P(None, "col"), P(), P())
    return jax.shard_map(
        functools.partial(local, mesh.shape["col"]),
        mesh=mesh,
        in_specs=placed,
        out_specs=(P(None, None, "row", "col"), P("col", None)),
        check_vma=False,
    )
```

```python
import functools

import jax
import jax.numpy as jnp
from jax import lax
from jax.experimental import pallas as pl
from jax.experimental.pallas import tpu as pltpu
from jax.sharding import PartitionSpec as P

MESH = pl.DeviceIdType.MESH
BANDS = 224
BLOCK = 128
SLOTS = 2
WIDE = SLOTS * BLOCK
TILE_H = 16
TILE_W = 128
PIX = TILE_H * TILE_W
PART = 32
SIZES = (32, 24)
CHIP = 56
ROWS = 8
COPIES = 4
ROW_ORDER = (4, 3, 5, 2, 6, 1, 7)
VMEM_LIMIT = 60 * 1024 * 1024
YS = 4
PAIR = 2 * TILE_W
PAIRS = PIX // PAIR
STEP = 0.2
THRESHOLD = 0.05
F32 = jnp.float32
BF16 = jnp.bfloat16


def nn(a, b):
    return lax.dot_general(a, b, (((1,), (0,)), ((), ())), preferred_element_type=F32)


def nt(a, b):
    return lax.dot_general(a, b, (((1,), (1,)), ((), ())), preferred_element_type=F32)


def split(x):
    hi = x.astype(BF16)
    return hi, (x - hi.astype(F32)).astype(BF16)


def start_of(row):
    return row // 2 * CHIP + row % 2 * PART


def kernel(
    cols, pix_hbm, lib_hbm, ids_hbm, counts_hbm, abund_hbm, lgrad_hbm,
    pix, ids, counts, lhi, llo, gath, bsend, spec, a1, a2, a3, ones,
    rs, rr, hs, hr, cs, cr, gsend, grecv, gacc, gn, gy, gzs, gz, obuf, lgrad,
    send_z, recv_z, send_y, recv_y, send_b, recv_b, send_h, recv_h, send_k, recv_k, send_g, recv_g,
    send_n, recv_n, send_ty, recv_ty, send_tz, recv_tz, send_c, recv_c, sem_in, sem_out,
):
    ny = YS
    nz = cols // ny
    r = lax.axis_index("row")
    c = lax.axis_index("col")
    z = c // ny
    y = lax.rem(c, ny)
    begin = pl.multiple_of(r // 2 * CHIP + lax.rem(r, 2) * PART, 8)

    def by_core(work):
        for k, size in enumerate(SIZES):
            pl.when(lax.rem(r, 2) == k)(functools.partial(work, size))

    def mine(size):
        return pl.ds(begin, size)

    near_first = sorted(range(1, nz), key=lambda d: (min(d, nz - d), d))
    place = {d: i for i, d in enumerate([0] + near_first)}
    rings = [[0]] + [[d for d in near_first if min(d, nz - d) == g] for g in range(1, nz // 2 + 1)]

    def span(g):
        return pl.ds(place[rings[g][0]], len(rings[g]))

    def far(src, dst, ssem, rsem, dev):
        return pltpu.make_async_remote_copy(
            src_ref=src, dst_ref=dst, send_sem=ssem, recv_sem=rsem,
            device_id=dev, device_id_type=MESH,
        )

    def on_z(d):
        return (r, lax.rem(z + d, nz) * ny + y)

    def on_y(e):
        return (r, z * ny + lax.rem(y + e, ny))

    def on_row(k):
        return (lax.rem(r + k, ROWS), c)

    pix_in = pltpu.make_async_copy(pix_hbm, pix, sem_in.at[0])
    ids_in = pltpu.make_async_copy(ids_hbm, ids, sem_in.at[1])
    counts_in = pltpu.make_async_copy(counts_hbm, counts, sem_in.at[2])

    def lib_in(size):
        return pltpu.make_async_copy(
            lib_hbm.at[mine(size)], gath.at[y, 0, pl.ds(0, size)], sem_in.at[3]
        )

    by_core(lambda size: lib_in(size).start())
    ids_in.start()
    counts_in.start()
    pix_in.start()

    barrier = pltpu.get_barrier_semaphore()

    def greet(dev):
        pl.semaphore_signal(barrier, inc=1, device_id=dev, device_id_type=MESH)

    for d in near_first[::-1]:
        greet(on_z(d))
    for k in ROW_ORDER:
        greet(on_row(k))
    for e in range(1, ny):
        greet(on_y(e))

    @pl.when(c > 0)
    def _():
        greet((r, c - 1))

    @pl.when(c < cols - 1)
    def _():
        greet((r, c + 1))

    corners = ((-1, -1, 0, 3), (1, -1, TILE_H - 1, 2), (-1, 1, TILE_H, 1), (1, 1, 2 * TILE_H - 1, 0))

    def within(dr, dc):
        return (r + dr >= 0) & (r + dr < ROWS) & (c + dc >= 0) & (c + dc < cols)

    across = jnp.int32(0)
    for dr, dc, _, _ in corners:
        across = across + within(dr, dc).astype(jnp.int32)

        @pl.when(within(dr, dc))
        def _():
            greet((r + dr, c + dc))

    beside_cols = (c > 0).astype(jnp.int32) + (c < cols - 1).astype(jnp.int32)
    pl.semaphore_wait(barrier, nz - 1 + ny - 1 + ROWS - 1 + beside_cols + across)

    def lib_z(size, d):
        rows = pl.ds(0, size)
        return far(gath.at[y, 0, rows], gath.at[y, place[d], rows], send_z.at[d], recv_z.at[d], on_z(d))

    def lib_y(size, g, e):
        block = gath.at[y, span(g), pl.ds(0, size)]
        return far(block, block, send_y.at[g, e], recv_y.at[g, e], on_y(e))

    @by_core
    def _(size):
        lib_in(size).wait()
        for d in near_first:
            lib_z(size, d).start()
        for e in range(1, ny):
            lib_y(size, 0, e).start()

    lane = lax.broadcasted_iota(jnp.int32, (64, PIX), 1)
    which = lax.rem(lax.broadcasted_iota(jnp.int32, (64, PIX), 0), 32)
    spot = jnp.where(which < TILE_H, which * TILE_W, (which - TILE_H) * TILE_W + TILE_W - 1)
    ones[...] = jnp.where(lane == spot, 1.0, 0.0).astype(BF16)

    @pl.when(r == 0)
    def _():
        for i in range(2):
            rr[i, 0] = jnp.zeros((WIDE, TILE_W), F32)

    @pl.when(r == ROWS - 1)
    def _():
        for i in range(2):
            rr[i, 1] = jnp.zeros((WIDE, TILE_W), F32)

    @pl.when(c == 0)
    def _():
        for i in range(2):
            hr[i, :TILE_H] = jnp.zeros((TILE_H, WIDE), F32)

    @pl.when(c == cols - 1)
    def _():
        for i in range(2):
            hr[i, TILE_H:] = jnp.zeros((TILE_H, WIDE), F32)

    for dr, dc, _, spot_at in corners:
        @pl.when(jnp.logical_not(within(dr, dc)))
        def _():
            cr[3 - spot_at] = jnp.zeros((8, WIDE), F32)

    pix_in.wait()
    for h in range(TILE_H):
        hi, lo = split(pix[pl.ds(h, BANDS, TILE_H), :])
        lhi[WIDE:, h * TILE_W:(h + 1) * TILE_W] = hi
        llo[WIDE:, h * TILE_W:(h + 1) * TILE_W] = lo
    ids_in.wait()
    counts_in.wait()

    def choose(size, row, s):
        block = ids[row, s, c]
        use = jnp.where(counts[row, c] > s, 1.0, 0.0)
        d = lax.rem(z - block // ny + nz, nz)
        at = jnp.where(d <= nz // 2, jnp.maximum(2 * d - 1, 0), 2 * (nz - d))
        return gath[lax.rem(block, ny), at, :size] * use

    def spec_copy(size, k):
        return far(
            bsend.at[k, :, pl.ds(0, size)], spec.at[:, mine(size), :], send_b.at[k], recv_b.at[r], on_row(k)
        )

    @by_core
    def _(size):
        for g in range(1, len(rings)):
            for d in rings[g]:
                lib_z(size, d).wait_recv()
            for e in sorted(range(1, ny), key=lambda e: -min(e, ny - e)):
                lib_y(size, g, e).start()
        for g in range(len(rings)):
            for e in range(1, ny):
                lib_y(size, g, e).wait_recv()
        for k in ROW_ORDER:
            for s in range(SLOTS):
                bsend[k, s, :size] = choose(size, lax.rem(r + k, ROWS), s)
            spec_copy(size, k).start()
        for s in range(SLOTS):
            spec[s, mine(size), :] = choose(size, r, s)

    for p in range(ROWS):
        @pl.when(r != p)
        def _():
            size = SIZES[p % 2]
            part = pl.ds(start_of(p), size)
            far(bsend.at[0, :, pl.ds(0, size)], spec.at[:, part, :], send_b.at[0], recv_b.at[p], (r, c)).wait_recv()

    spectra = jnp.concatenate([spec[0], spec[1]], axis=1)
    s_hi, s_lo = split(spectra)
    t_hi, t_lo = split(spectra.T)

    def lanes(j, pad=0):
        return slice(j * PAIR + pad, (j + 1) * PAIR + pad)

    def keep(j, value):
        hi, lo = split(value)
        lhi[:WIDE, lanes(j)] = hi
        llo[:WIDE, lanes(j)] = lo

    def row_copies(i):
        up = far(rs.at[i, 0], rr.at[i, 1], send_h.at[i, 2], recv_h.at[i, 3], (r - 1, c))
        down = far(rs.at[i, 1], rr.at[i, 0], send_h.at[i, 3], recv_h.at[i, 2], (r + 1, c))
        return up, down

    def col_copies(i):
        left = far(hs.at[i, :TILE_H], hr.at[i, TILE_H:], send_h.at[i, 0], recv_h.at[i, 1], (r, c - 1))
        right = far(hs.at[i, TILE_H:], hr.at[i, :TILE_H], send_h.at[i, 1], recv_h.at[i, 0], (r, c + 1))
        return left, right

    def act(low, high, pos, count, what):
        @pl.when(pos > 0)
        def _():
            if what == "start":
                low.start()
            elif what == "send":
                low.wait_send()
            else:
                high.wait_recv()

        @pl.when(pos < count - 1)
        def _():
            if what == "start":
                high.start()
            elif what == "send":
                high.wait_send()
            else:
                low.wait_recv()

    def edge_rows(i, what):
        act(*row_copies(i), r, ROWS, what)

    def edge_cols(i, what):
        act(*col_copies(i), c, cols, what)

    def pack(i):
        picked = ones[:32, :]
        hs[i] = nt(picked, lhi[:WIDE, :]) + nt(picked, llo[:WIDE, :])

    def corner_copy(i):
        dr, dc, _, spot_at = corners[i]
        return far(cs.at[i], cr.at[spot_at], send_k.at[i], recv_k.at[spot_at], (r + dr, c + dc))

    def edge_corners(what):
        for i, (dr, dc, row, _) in enumerate(corners):
            @pl.when(within(dr, dc))
            def _():
                if what == "start":
                    cs[i] = jnp.broadcast_to(hs[0, row:row + 1, :], (8, WIDE))
                    corner_copy(i).start()
                elif what == "send":
                    corner_copy(i).wait_send()
                else:
                    corner_copy(3 - i).wait_recv()

    def first(j):
        p_hi = lhi[WIDE:, lanes(j)]
        p_lo = llo[WIDE:, lanes(j)]
        value = STEP * (nn(t_hi, p_hi) + nn(t_hi, p_lo) + nn(t_lo, p_hi))
        a1[:, lanes(j)] = value
        keep(j, value)
        return value

    rim = [0, PAIRS - 1]
    rs[0, 0] = first(0)[:, :TILE_W]
    rs[0, 1] = first(PAIRS - 1)[:, TILE_W:]
    edge_rows(0, "start")
    for j in (1, PAIRS - 2):
        first(j)


    gram = nn(t_hi, s_hi) + nn(t_hi, s_lo) + nn(t_lo, s_hi)
    gi = lax.broadcasted_iota(jnp.int32, (WIDE, WIDE), 0)
    gj = lax.broadcasted_iota(jnp.int32, (WIDE, WIDE), 1)
    u_hi, u_lo = split(jnp.where(gi == gj, 0.4, 0.0) - STEP * gram)
    column = lax.broadcasted_iota(jnp.int32, (WIDE, TILE_W), 1)

    def beside(own):
        halves = []
        for q in range(2):
            x = own[:, q * TILE_W:(q + 1) * TILE_W]
            from_left = jnp.where(column == 0, 0.0, pltpu.roll(x, 1, 1))
            from_right = jnp.where(column == TILE_W - 1, 0.0, pltpu.roll(x, TILE_W - 1, 1))
            halves.append(from_left + from_right)
        return jnp.concatenate(halves, axis=1)

    blank = jnp.zeros((WIDE, TILE_W), F32)

    def inner(j, a, excess):
        own = a[:, lanes(j)]
        a_hi = lhi[:WIDE, lanes(j)]
        a_lo = llo[:WIDE, lanes(j)]
        value = nn(u_hi, a_hi) + nn(u_hi, a_lo) + nn(u_lo, a_hi)
        value = value + a1[:, lanes(j)] + STEP * (jnp.abs(excess) - THRESHOLD)
        if j == 0:
            above = jnp.concatenate([blank, a[:, :TILE_W]], axis=1)
        else:
            above = a[:, lanes(j, -TILE_W)]
        if j == PAIRS - 1:
            below = jnp.concatenate([a[:, PIX - TILE_W:], blank], axis=1)
        else:
            below = a[:, lanes(j, TILE_W)]
        return value + 0.1 * (beside(own) + above + below)

    def columns(edge):
        hi, lo = split(edge)
        return jnp.concatenate([hi.astype(F32), lo.astype(F32)], axis=0).T.astype(BF16)

    def outer(j, side, above, below):
        value = nn(side, ones[:, lanes(j)])
        if j == 0:
            value = value + jnp.concatenate([above, blank], axis=1)
        if j == PAIRS - 1:
            value = value + jnp.concatenate([blank, below], axis=1)
        return 0.1 * value

    def second(j):
        value = inner(j, a1, a1[:, lanes(j)] - THRESHOLD)
        a2[:, lanes(j)] = value
        return value

    rs[1, 0] = second(0)[:, :TILE_W]
    rs[1, 1] = second(PAIRS - 1)[:, TILE_W:]
    edge_rows(1, "start")
    for j in range(2, PAIRS - 2):
        first(j)
    pack(0)
    edge_cols(0, "start")
    edge_corners("start")
    for j in range(1, PAIRS - 1):
        keep(j, second(j))
    for j in rim:
        keep(j, a2[:, lanes(j)])
    pack(1)
    edge_cols(1, "start")
    edge_rows(0, "recv")
    edge_cols(0, "recv")
    side1 = columns(hr[0])
    for j in range(PAIRS):
        value = a2[:, lanes(j)] + outer(j, side1, rr[0, 0], rr[0, 1])
        a2[:, lanes(j)] = value
        keep(j, value)
    for j in range(PAIRS):
        excess = a2[:, lanes(j)] + jnp.minimum(a1[:, lanes(j)] - THRESHOLD, 0.0)
        a3[:, lanes(j)] = inner(j, a2, excess)
    edge_rows(1, "recv")
    edge_cols(1, "recv")
    edge_corners("recv")

    above2 = rr[1, 0] + jnp.where(r > 0, 0.1, 0.0) * a1[:, :TILE_W]
    below2 = rr[1, 1] + jnp.where(r < ROWS - 1, 0.1, 0.0) * a1[:, PIX - TILE_W:]
    row = lax.broadcasted_iota(jnp.int32, (2 * TILE_H, WIDE), 0)
    share = jnp.where(row < TILE_H, jnp.where(c > 0, 0.1, 0.0), jnp.where(c < cols - 1, 0.1, 0.0))
    edge2 = hr[1] + share * hs[0]
    for spot_at, at in enumerate((0, TILE_H - 1, TILE_H, 2 * TILE_H - 1)):
        edge2 = edge2 + jnp.where(row == at, 0.2 * cr[spot_at, :1, :], 0.0)
    side2 = columns(edge2)
    for j in range(PAIRS):
        value = a3[:, lanes(j)] + outer(j, side2, above2, below2)
        a3[:, lanes(j)] = value
        keep(j, value)

    both = (
        nt(lhi[...], lhi[:WIDE, :]) + nt(lhi[...], llo[:WIDE, :]) + nt(llo[...], lhi[:WIDE, :])
    )
    c_hi, c_lo = split(both[:WIDE])
    grad = nn(s_hi, c_hi) + nn(s_hi, c_lo) + nn(s_lo, c_hi) - both[WIDE:]
    for s in range(SLOTS):
        use = jnp.where(counts[r, c] > s, 1.0 / PIX, 0.0)
        gsend[s] = grad[:, s * BLOCK:(s + 1) * BLOCK] * use

    def grad_copy(size, k):
        other = SIZES[(SIZES.index(size) + k) % 2]
        row, _ = on_row(k)
        first = pl.multiple_of(row // 2 * CHIP + lax.rem(row, 2) * PART, 8)
        return far(
            gsend.at[:, pl.ds(first, other), :], grecv.at[r, :, pl.ds(0, other)],
            send_g.at[k], recv_g.at[r], on_row(k),
        )

    @by_core
    def _(size):
        for k in ROW_ORDER:
            grad_copy(size, k).start()
        grecv[r, :, :size] = gsend[:, mine(size), :]

    for h in range(TILE_H):
        obuf[pl.ds(h, WIDE, TILE_H), :] = a3[:, h * TILE_W:(h + 1) * TILE_W]
    abund_out = pltpu.make_async_copy(obuf, abund_hbm, sem_out.at[0])
    abund_out.start()

    beside_z = [1, nz - 1] if nz > 3 else []
    far_rings = [g for g in range(len(rings) - 1, 0, -1) if rings[g] != beside_z]
    far_first = [d for g in far_rings for d in rings[g]]

    def sum_n(size, i):
        rows = pl.ds(0, size)
        return far(
            gacc.at[:, place[beside_z[i]], rows], gn.at[i, :, rows], send_n.at[i], recv_n.at[i], on_z(beside_z[i])
        )

    def sum_y(size, g, e):
        rows = pl.ds(0, size)
        return far(
            gacc.at[e, span(g), rows], gy.at[e, span(g), rows], send_ty.at[g, e], recv_ty.at[g, e], on_y(e)
        )

    def sum_z(size, d):
        rows = pl.ds(0, size)
        return far(gzs.at[d, rows], gz.at[d, rows], send_tz.at[d], recv_tz.at[d], on_z(d))

    def part_copy(size, k):
        return far(
            lgrad.at[mine(size)], lgrad_hbm.at[mine(size)], send_c.at[k], recv_c.at[r], on_row(k)
        )

    def part_out(size):
        return pltpu.make_async_copy(lgrad.at[mine(size)], lgrad_hbm.at[mine(size)], sem_out.at[1])

    @by_core
    def _(size):
        for q in range(ROWS):
            @pl.when(r != q)
            def _():
                far(
                    gsend.at[:, pl.ds(0, size), :], grecv.at[q, :, pl.ds(0, size)],
                    send_g.at[0], recv_g.at[q], (q, c),
                ).wait_recv()

        named = [[ids[q, s, c] for s in range(SLOTS)] for q in range(ROWS)]

        def collect(d, e):
            owner = lax.rem(z + d, nz) * ny + lax.rem(y + e, ny)
            total = jnp.zeros((size, BLOCK), F32)
            for q in range(ROWS):
                for s in range(SLOTS):
                    total = total + jnp.where(named[q][s] == owner, 1.0, 0.0) * grecv[q, s, :size]
            return total

        others = sorted(range(1, ny), key=lambda e: -min(e, ny - e))
        for i, d in enumerate(beside_z):
            for e in range(ny):
                gacc[e, place[d], :size] = collect(d, e)
            sum_n(size, i).start()
        for g in far_rings:
            for e in others + [0]:
                for d in rings[g]:
                    gacc[e, place[d], :size] = collect(d, e)
                if e:
                    sum_y(size, g, e).start()

        def forward(g):
            for e in others:
                sum_y(size, g, e).wait_recv()
            for d in rings[g]:
                total = gacc[0, place[d], :size]
                for e in others:
                    total = total + gy[e, place[d], :size]
                if d:
                    gzs[d, :size] = total
                    sum_z(size, d).start()
            return total

        own = [collect(0, e) for e in range(ny)]
        for g in far_rings[:1]:
            forward(g)
        for i in range(len(beside_z)):
            sum_n(size, i).wait_recv()
            own = [own[e] + gn[i, e, :size] for e in range(ny)]
        for e in others + [0]:
            gacc[e, 0, :size] = own[e]
            if e:
                sum_y(size, 0, e).start()
        for g in far_rings[1:]:
            forward(g)
        total = forward(0)
        for d in far_first:
            sum_z(size, d).wait_recv()
            total = total + gz[d, :size]
        lgrad[mine(size), :] = total
        for k in ROW_ORDER:
            part_copy(size, k).start()
        part_out(size).start()

        for d in near_first:
            lib_z(size, d).wait_send()
        for g in range(len(rings)):
            for e in range(1, ny):
                lib_y(size, g, e).wait_send()
        for i in range(len(beside_z)):
            sum_n(size, i).wait_send()
        for d in far_first:
            sum_z(size, d).wait_send()
        for g in far_rings + [0]:
            for e in range(1, ny):
                sum_y(size, g, e).wait_send()
        for k in ROW_ORDER:
            spec_copy(size, k).wait_send()
            grad_copy(size, k).wait_send()

    for i in range(2):
        edge_rows(i, "send")
        edge_cols(i, "send")
    edge_corners("send")
    abund_out.wait()

    for p in range(ROWS):
        @pl.when(r != p)
        def _():
            part = pl.ds(start_of(p), SIZES[p % 2])
            far(lgrad.at[part], lgrad_hbm.at[part], send_c.at[0], recv_c.at[p], (r, c)).wait_recv()

    @by_core
    def _(size):
        part_out(size).wait()
        for k in ROW_ORDER:
            part_copy(size, k).wait_send()


def finish(abund_in, lgrad_in, abund_out, lgrad_out, abund, lgrad, sems_in, sems_out):
    rows = abund_in.shape[0] // COPIES
    ways = [(lgrad_in, lgrad, lgrad_out)]
    for i in range(COPIES):
        part = pl.ds(i * rows, rows)
        ways.append((abund_in.at[part], abund.at[part], abund_out.at[part]))
    reads = [pltpu.make_async_copy(way[0], way[1], sems_in.at[i]) for i, way in enumerate(ways)]
    writes = [pltpu.make_async_copy(way[1], way[2], sems_out.at[i]) for i, way in enumerate(ways)]
    for read in reads:
        read.start()
    for read, write in zip(reads, writes):
        read.wait()
        write.start()
    for write in writes:
        write.wait()


def local(cols, pixels, library, block_ids, counts):
    dma = pltpu.SemaphoreType.DMA
    ny = YS
    nz = cols // ny
    hbm = pl.BlockSpec(memory_space=pltpu.HBM)
    shapes = (
        jax.ShapeDtypeStruct((WIDE * TILE_H, TILE_W), F32),
        jax.ShapeDtypeStruct((BANDS, BLOCK), F32),
    )
    abundance, grad = pl.pallas_call(
        functools.partial(kernel, cols),
        out_shape=shapes,
        in_specs=[hbm] * 4,
        out_specs=(hbm, hbm),
        scratch_shapes=[
            pltpu.VMEM((BANDS * TILE_H, TILE_W), F32),
            pltpu.SMEM((ROWS, SLOTS, cols), jnp.int32),
            pltpu.SMEM((ROWS, cols), jnp.int32),
            pltpu.VMEM((WIDE + BANDS, PIX), BF16),
            pltpu.VMEM((WIDE + BANDS, PIX), BF16),
            pltpu.VMEM((ny, nz, PART, BLOCK), F32),
            pltpu.VMEM((ROWS, SLOTS, PART, BLOCK), F32),
            pltpu.VMEM((SLOTS, BANDS, BLOCK), F32),
            pltpu.VMEM((WIDE, PIX), F32),
            pltpu.VMEM((WIDE, PIX), F32),
            pltpu.VMEM((WIDE, PIX), F32),
            pltpu.VMEM((64, PIX), BF16),
            pltpu.VMEM((2, 2, WIDE, TILE_W), F32),
            pltpu.VMEM((2, 2, WIDE, TILE_W), F32),
            pltpu.VMEM((2, 32, WIDE), F32),
            pltpu.VMEM((2, 32, WIDE), F32),
            pltpu.VMEM((4, 8, WIDE), F32),
            pltpu.VMEM((4, 8, WIDE), F32),
            pltpu.VMEM((SLOTS, BANDS, BLOCK), F32),
            pltpu.VMEM((ROWS, SLOTS, PART, BLOCK), F32),
            pltpu.VMEM((ny, nz, PART, BLOCK), F32),
            pltpu.VMEM((2, ny, PART, BLOCK), F32),
            pltpu.VMEM((ny, nz, PART, BLOCK), F32),
            pltpu.VMEM((nz, PART, BLOCK), F32),
            pltpu.VMEM((nz, PART, BLOCK), F32),
            pltpu.VMEM((WIDE * TILE_H, TILE_W), F32),
            pltpu.VMEM((BANDS, BLOCK), F32),
            dma((nz,)), dma((nz,)),
            dma((nz, ny)), dma((nz, ny)),
            dma((ROWS,)), dma((ROWS,)),
            dma((2, 4)), dma((2, 4)),
            dma((4,)), dma((4,)),
            dma((ROWS,)), dma((ROWS,)),
            dma((2,)), dma((2,)),
            dma((nz, ny)), dma((nz, ny)),
            dma((nz,)), dma((nz,)),
            dma((ROWS,)), dma((ROWS,)),
            dma((4,)), dma((2,)),
        ],
        compiler_params=pltpu.CompilerParams(
            collective_id=0, has_side_effects=True, vmem_limit_bytes=VMEM_LIMIT
        ),
    )(
        pixels.reshape(BANDS * TILE_H, TILE_W), library,
        block_ids.transpose(0, 2, 1), counts,
    )
    abundance, grad = pl.pallas_call(
        finish,
        out_shape=shapes,
        in_specs=[hbm, hbm],
        out_specs=(hbm, hbm),
        scratch_shapes=[
            pltpu.VMEM((WIDE * TILE_H, TILE_W), F32),
            pltpu.VMEM((BANDS, BLOCK), F32),
            dma((COPIES + 1,)), dma((COPIES + 1,)),
        ],
        compiler_params=pltpu.CompilerParams(vmem_limit_bytes=VMEM_LIMIT),
    )(abundance, grad)
    return abundance.reshape(SLOTS, BLOCK, TILE_H, TILE_W), grad.T


def solution(mesh):
    placed = (P(None, "row", "col"), P(None, "col"), P(), P())
    return jax.shard_map(
        functools.partial(local, mesh.shape["col"]),
        mesh=mesh,
        in_specs=placed,
        out_specs=(P(None, None, "row", "col"), P("col", None)),
        check_vma=False,
    )
```

```python
import functools

import jax
import jax.numpy as jnp
from jax import lax
from jax.experimental import pallas as pl
from jax.experimental.pallas import tpu as pltpu
from jax.sharding import PartitionSpec as P

MESH = pl.DeviceIdType.MESH
BANDS = 224
BLOCK = 128
SLOTS = 2
WIDE = SLOTS * BLOCK
TILE_H = 16
TILE_W = 128
PIX = TILE_H * TILE_W
PART = 32
SIZES = (32, 24)
CHIP = 56
ROWS = 8
COPIES = 4
ROW_ORDER = (4, 3, 5, 2, 6, 1, 7)
VMEM_LIMIT = 60 * 1024 * 1024
YS = 4
PAIR = 2 * TILE_W
PAIRS = PIX // PAIR
STEP = 0.2
THRESHOLD = 0.05
F32 = jnp.float32
BF16 = jnp.bfloat16


def nn(a, b):
    return lax.dot_general(a, b, (((1,), (0,)), ((), ())), preferred_element_type=F32)


def nt(a, b):
    return lax.dot_general(a, b, (((1,), (1,)), ((), ())), preferred_element_type=F32)


def split(x):
    hi = x.astype(BF16)
    return hi, (x - hi.astype(F32)).astype(BF16)


def start_of(row):
    return row // 2 * CHIP + row % 2 * PART


def kernel(
    cols, pix_hbm, lib_hbm, ids_hbm, counts_hbm, abund_hbm, lgrad_hbm,
    pix, ids, counts, lhi, llo, gath, bsend, spec, a1, a2, a3, ones,
    rs, rr, hs, hr, cs, cr, gsend, grecv, gacc, gn, gy, gzs, gz, obuf, lgrad,
    send_z, recv_z, send_y, recv_y, send_b, recv_b, send_h, recv_h, send_k, recv_k, send_g, recv_g,
    send_n, recv_n, send_ty, recv_ty, send_tz, recv_tz, send_c, recv_c, sem_in, sem_out,
):
    ny = YS
    nz = cols // ny
    r = lax.axis_index("row")
    c = lax.axis_index("col")
    z = c // ny
    y = lax.rem(c, ny)
    begin = pl.multiple_of(r // 2 * CHIP + lax.rem(r, 2) * PART, 8)

    def by_core(work):
        for k, size in enumerate(SIZES):
            pl.when(lax.rem(r, 2) == k)(functools.partial(work, size))

    def mine(size):
        return pl.ds(begin, size)

    near_first = sorted(range(1, nz), key=lambda d: (min(d, nz - d), d))
    place = {d: i for i, d in enumerate([0] + near_first)}
    rings = [[0]] + [[d for d in near_first if min(d, nz - d) == g] for g in range(1, nz // 2 + 1)]

    def span(g):
        return pl.ds(place[rings[g][0]], len(rings[g]))

    def far(src, dst, ssem, rsem, dev):
        return pltpu.make_async_remote_copy(
            src_ref=src, dst_ref=dst, send_sem=ssem, recv_sem=rsem,
            device_id=dev, device_id_type=MESH,
        )

    def on_z(d):
        return (r, lax.rem(z + d, nz) * ny + y)

    def on_y(e):
        return (r, z * ny + lax.rem(y + e, ny))

    def on_row(k):
        return (lax.rem(r + k, ROWS), c)

    pix_in = pltpu.make_async_copy(pix_hbm, pix, sem_in.at[0])
    ids_in = pltpu.make_async_copy(ids_hbm, ids, sem_in.at[1])
    counts_in = pltpu.make_async_copy(counts_hbm, counts, sem_in.at[2])

    def lib_in(size):
        return pltpu.make_async_copy(
            lib_hbm.at[mine(size)], gath.at[y, 0, pl.ds(0, size)], sem_in.at[3]
        )

    by_core(lambda size: lib_in(size).start())
    ids_in.start()
    counts_in.start()
    pix_in.start()

    barrier = pltpu.get_barrier_semaphore()

    def greet(dev):
        pl.semaphore_signal(barrier, inc=1, device_id=dev, device_id_type=MESH)

    for d in near_first[::-1]:
        greet(on_z(d))
    for k in ROW_ORDER:
        greet(on_row(k))
    for e in range(1, ny):
        greet(on_y(e))

    to_left = (c > 0) & (y == 0)
    to_right = (c < cols - 1) & (y == ny - 1)

    @pl.when(to_left)
    def _():
        greet((r, c - 1))

    @pl.when(to_right)
    def _():
        greet((r, c + 1))

    corners = ((-1, -1, 0, 3), (1, -1, TILE_H - 1, 2), (-1, 1, TILE_H, 1), (1, 1, 2 * TILE_H - 1, 0))

    def within(dr, dc):
        return (r + dr >= 0) & (r + dr < ROWS) & (c + dc >= 0) & (c + dc < cols)

    across = jnp.int32(0)
    for dr, dc, _, _ in corners:
        across = across + within(dr, dc).astype(jnp.int32)

        @pl.when(within(dr, dc))
        def _():
            greet((r + dr, c + dc))

    beside_cols = to_left.astype(jnp.int32) + to_right.astype(jnp.int32)
    pl.semaphore_wait(barrier, nz - 1 + ny - 1 + ROWS - 1 + beside_cols + across)

    def lib_z(size, d):
        rows = pl.ds(0, size)
        return far(gath.at[y, 0, rows], gath.at[y, place[d], rows], send_z.at[d], recv_z.at[d], on_z(d))

    def lib_y(size, g, e):
        block = gath.at[y, span(g), pl.ds(0, size)]
        return far(block, block, send_y.at[g, e], recv_y.at[g, e], on_y(e))

    @by_core
    def _(size):
        lib_in(size).wait()
        for d in near_first:
            lib_z(size, d).start()
        for e in range(1, ny):
            lib_y(size, 0, e).start()

    lane = lax.broadcasted_iota(jnp.int32, (64, PIX), 1)
    which = lax.rem(lax.broadcasted_iota(jnp.int32, (64, PIX), 0), 32)
    spot = jnp.where(which < TILE_H, which * TILE_W, (which - TILE_H) * TILE_W + TILE_W - 1)
    ones[...] = jnp.where(lane == spot, 1.0, 0.0).astype(BF16)

    @pl.when(r == 0)
    def _():
        for i in range(2):
            rr[i, 0] = jnp.zeros((WIDE, TILE_W), F32)

    @pl.when(r == ROWS - 1)
    def _():
        for i in range(2):
            rr[i, 1] = jnp.zeros((WIDE, TILE_W), F32)

    @pl.when(c == 0)
    def _():
        for i in range(2):
            hr[i, :TILE_H] = jnp.zeros((TILE_H, WIDE), F32)

    @pl.when(c == cols - 1)
    def _():
        for i in range(2):
            hr[i, TILE_H:] = jnp.zeros((TILE_H, WIDE), F32)

    for dr, dc, _, spot_at in corners:
        @pl.when(jnp.logical_not(within(dr, dc)))
        def _():
            cr[3 - spot_at] = jnp.zeros((8, WIDE), F32)

    pix_in.wait()
    for h in range(TILE_H):
        hi, lo = split(pix[pl.ds(h, BANDS, TILE_H), :])
        lhi[WIDE:, h * TILE_W:(h + 1) * TILE_W] = hi
        llo[WIDE:, h * TILE_W:(h + 1) * TILE_W] = lo
    ids_in.wait()
    counts_in.wait()

    def choose(size, row, s):
        block = ids[row, s, c]
        use = jnp.where(counts[row, c] > s, 1.0, 0.0)
        d = lax.rem(z - block // ny + nz, nz)
        at = jnp.where(d <= nz // 2, jnp.maximum(2 * d - 1, 0), 2 * (nz - d))
        return gath[lax.rem(block, ny), at, :size] * use

    def spec_copy(size, k):
        return far(
            bsend.at[k, :, pl.ds(0, size)], spec.at[:, mine(size), :], send_b.at[k], recv_b.at[r], on_row(k)
        )

    @by_core
    def _(size):
        for g in range(1, len(rings)):
            for d in rings[g]:
                lib_z(size, d).wait_recv()
            for e in sorted(range(1, ny), key=lambda e: -min(e, ny - e)):
                lib_y(size, g, e).start()
        for g in range(len(rings)):
            for e in range(1, ny):
                lib_y(size, g, e).wait_recv()
        for k in ROW_ORDER:
            for s in range(SLOTS):
                bsend[k, s, :size] = choose(size, lax.rem(r + k, ROWS), s)
            spec_copy(size, k).start()
        for s in range(SLOTS):
            spec[s, mine(size), :] = choose(size, r, s)

    for p in range(ROWS):
        @pl.when(r != p)
        def _():
            size = SIZES[p % 2]
            part = pl.ds(start_of(p), size)
            far(bsend.at[0, :, pl.ds(0, size)], spec.at[:, part, :], send_b.at[0], recv_b.at[p], (r, c)).wait_recv()

    spectra = jnp.concatenate([spec[0], spec[1]], axis=1)
    s_hi, s_lo = split(spectra)
    t_hi, t_lo = split(spectra.T)

    def lanes(j, pad=0):
        return slice(j * PAIR + pad, (j + 1) * PAIR + pad)

    def keep(j, value):
        hi, lo = split(value)
        lhi[:WIDE, lanes(j)] = hi
        llo[:WIDE, lanes(j)] = lo

    def row_copies(i):
        up = far(rs.at[i, 0], rr.at[i, 1], send_h.at[i, 2], recv_h.at[i, 3], (r - 1, c))
        down = far(rs.at[i, 1], rr.at[i, 0], send_h.at[i, 3], recv_h.at[i, 2], (r + 1, c))
        return up, down

    def col_copies(i):
        left = far(hs.at[i, :TILE_H], hr.at[i, TILE_H:], send_h.at[i, 0], recv_h.at[i, 1], (r, c - 1))
        right = far(hs.at[i, TILE_H:], hr.at[i, :TILE_H], send_h.at[i, 1], recv_h.at[i, 0], (r, c + 1))
        return left, right

    def act(low, high, pos, count, what):
        @pl.when(pos > 0)
        def _():
            if what == "start":
                low.start()
            elif what == "send":
                low.wait_send()
            else:
                high.wait_recv()

        @pl.when(pos < count - 1)
        def _():
            if what == "start":
                high.start()
            elif what == "send":
                high.wait_send()
            else:
                low.wait_recv()

    def edge_rows(i, what):
        act(*row_copies(i), r, ROWS, what)

    def edge_cols(i, what):
        act(*col_copies(i), c, cols, what)

    def pack(i):
        picked = ones[:32, :]
        hs[i] = nt(picked, lhi[:WIDE, :]) + nt(picked, llo[:WIDE, :])

    def corner_copy(i):
        dr, dc, _, spot_at = corners[i]
        return far(cs.at[i], cr.at[spot_at], send_k.at[i], recv_k.at[spot_at], (r + dr, c + dc))

    def edge_corners(what):
        for i, (dr, dc, row, _) in enumerate(corners):
            @pl.when(within(dr, dc))
            def _():
                if what == "start":
                    cs[i] = jnp.broadcast_to(hs[0, row:row + 1, :], (8, WIDE))
                    corner_copy(i).start()
                elif what == "send":
                    corner_copy(i).wait_send()
                else:
                    corner_copy(3 - i).wait_recv()

    def first(j):
        p_hi = lhi[WIDE:, lanes(j)]
        p_lo = llo[WIDE:, lanes(j)]
        value = STEP * (nn(t_hi, p_hi) + nn(t_hi, p_lo) + nn(t_lo, p_hi))
        a1[:, lanes(j)] = value
        keep(j, value)
        return value

    rim = [0, PAIRS - 1]
    rs[0, 0] = first(0)[:, :TILE_W]
    rs[0, 1] = first(PAIRS - 1)[:, TILE_W:]
    edge_rows(0, "start")
    for j in (1, PAIRS - 2):
        first(j)


    gram = nn(t_hi, s_hi) + nn(t_hi, s_lo) + nn(t_lo, s_hi)
    gi = lax.broadcasted_iota(jnp.int32, (WIDE, WIDE), 0)
    gj = lax.broadcasted_iota(jnp.int32, (WIDE, WIDE), 1)
    u_hi, u_lo = split(jnp.where(gi == gj, 0.4, 0.0) - STEP * gram)
    column = lax.broadcasted_iota(jnp.int32, (WIDE, TILE_W), 1)

    def beside(own):
        halves = []
        for q in range(2):
            x = own[:, q * TILE_W:(q + 1) * TILE_W]
            from_left = jnp.where(column == 0, 0.0, pltpu.roll(x, 1, 1))
            from_right = jnp.where(column == TILE_W - 1, 0.0, pltpu.roll(x, TILE_W - 1, 1))
            halves.append(from_left + from_right)
        return jnp.concatenate(halves, axis=1)

    blank = jnp.zeros((WIDE, TILE_W), F32)

    def inner(j, a, excess):
        own = a[:, lanes(j)]
        a_hi = lhi[:WIDE, lanes(j)]
        a_lo = llo[:WIDE, lanes(j)]
        value = nn(u_hi, a_hi) + nn(u_hi, a_lo) + nn(u_lo, a_hi)
        value = value + a1[:, lanes(j)] + STEP * (jnp.abs(excess) - THRESHOLD)
        if j == 0:
            above = jnp.concatenate([blank, a[:, :TILE_W]], axis=1)
        else:
            above = a[:, lanes(j, -TILE_W)]
        if j == PAIRS - 1:
            below = jnp.concatenate([a[:, PIX - TILE_W:], blank], axis=1)
        else:
            below = a[:, lanes(j, TILE_W)]
        return value + 0.1 * (beside(own) + above + below)

    def columns(edge):
        hi, lo = split(edge)
        return jnp.concatenate([hi.astype(F32), lo.astype(F32)], axis=0).T.astype(BF16)

    def outer(j, side, above, below):
        value = nn(side, ones[:, lanes(j)])
        if j == 0:
            value = value + jnp.concatenate([above, blank], axis=1)
        if j == PAIRS - 1:
            value = value + jnp.concatenate([blank, below], axis=1)
        return 0.1 * value

    def second(j):
        value = inner(j, a1, a1[:, lanes(j)] - THRESHOLD)
        a2[:, lanes(j)] = value
        return value

    rs[1, 0] = second(0)[:, :TILE_W]
    rs[1, 1] = second(PAIRS - 1)[:, TILE_W:]
    edge_rows(1, "start")
    for j in range(2, PAIRS - 2):
        first(j)
    pack(0)
    edge_cols(0, "start")
    edge_corners("start")
    for j in range(1, PAIRS - 1):
        keep(j, second(j))
    for j in rim:
        keep(j, a2[:, lanes(j)])
    pack(1)
    edge_cols(1, "start")
    edge_rows(0, "recv")
    edge_cols(0, "recv")
    side1 = columns(hr[0])
    for j in range(PAIRS):
        value = a2[:, lanes(j)] + outer(j, side1, rr[0, 0], rr[0, 1])
        a2[:, lanes(j)] = value
        keep(j, value)
    for j in range(PAIRS):
        excess = a2[:, lanes(j)] + jnp.minimum(a1[:, lanes(j)] - THRESHOLD, 0.0)
        a3[:, lanes(j)] = inner(j, a2, excess)
    edge_rows(1, "recv")
    edge_cols(1, "recv")
    edge_corners("recv")

    above2 = rr[1, 0] + jnp.where(r > 0, 0.1, 0.0) * a1[:, :TILE_W]
    below2 = rr[1, 1] + jnp.where(r < ROWS - 1, 0.1, 0.0) * a1[:, PIX - TILE_W:]
    row = lax.broadcasted_iota(jnp.int32, (2 * TILE_H, WIDE), 0)
    share = jnp.where(row < TILE_H, jnp.where(c > 0, 0.1, 0.0), jnp.where(c < cols - 1, 0.1, 0.0))
    edge2 = hr[1] + share * hs[0]
    for spot_at, at in enumerate((0, TILE_H - 1, TILE_H, 2 * TILE_H - 1)):
        edge2 = edge2 + jnp.where(row == at, 0.2 * cr[spot_at, :1, :], 0.0)
    side2 = columns(edge2)
    for j in range(PAIRS):
        value = a3[:, lanes(j)] + outer(j, side2, above2, below2)
        a3[:, lanes(j)] = value
        keep(j, value)

    both = (
        nt(lhi[...], lhi[:WIDE, :]) + nt(lhi[...], llo[:WIDE, :]) + nt(llo[...], lhi[:WIDE, :])
    )
    c_hi, c_lo = split(both[:WIDE])
    grad = nn(s_hi, c_hi) + nn(s_hi, c_lo) + nn(s_lo, c_hi) - both[WIDE:]
    for s in range(SLOTS):
        use = jnp.where(counts[r, c] > s, 1.0 / PIX, 0.0)
        gsend[s] = grad[:, s * BLOCK:(s + 1) * BLOCK] * use

    def grad_copy(size, k):
        other = SIZES[(SIZES.index(size) + k) % 2]
        row, _ = on_row(k)
        first = pl.multiple_of(row // 2 * CHIP + lax.rem(row, 2) * PART, 8)
        return far(
            gsend.at[:, pl.ds(first, other), :], grecv.at[r, :, pl.ds(0, other)],
            send_g.at[k], recv_g.at[r], on_row(k),
        )

    @by_core
    def _(size):
        for k in ROW_ORDER:
            grad_copy(size, k).start()
        grecv[r, :, :size] = gsend[:, mine(size), :]

    for h in range(TILE_H):
        obuf[pl.ds(h, WIDE, TILE_H), :] = a3[:, h * TILE_W:(h + 1) * TILE_W]
    abund_out = pltpu.make_async_copy(obuf, abund_hbm, sem_out.at[0])
    abund_out.start()

    beside_z = [1, nz - 1] if nz > 3 else []
    far_rings = [g for g in range(len(rings) - 1, 0, -1) if rings[g] != beside_z]
    far_first = [d for g in far_rings for d in rings[g]]

    def sum_n(size, i):
        rows = pl.ds(0, size)
        return far(
            gacc.at[:, place[beside_z[i]], rows], gn.at[i, :, rows], send_n.at[i], recv_n.at[i], on_z(beside_z[i])
        )

    def sum_y(size, g, e):
        rows = pl.ds(0, size)
        return far(
            gacc.at[e, span(g), rows], gy.at[e, span(g), rows], send_ty.at[g, e], recv_ty.at[g, e], on_y(e)
        )

    def sum_z(size, d):
        rows = pl.ds(0, size)
        return far(gzs.at[d, rows], gz.at[d, rows], send_tz.at[d], recv_tz.at[d], on_z(d))

    def part_copy(size, k):
        return far(
            lgrad.at[mine(size)], lgrad_hbm.at[mine(size)], send_c.at[k], recv_c.at[r], on_row(k)
        )

    def part_out(size):
        return pltpu.make_async_copy(lgrad.at[mine(size)], lgrad_hbm.at[mine(size)], sem_out.at[1])

    @by_core
    def _(size):
        for q in range(ROWS):
            @pl.when(r != q)
            def _():
                far(
                    gsend.at[:, pl.ds(0, size), :], grecv.at[q, :, pl.ds(0, size)],
                    send_g.at[0], recv_g.at[q], (q, c),
                ).wait_recv()

        named = [[ids[q, s, c] for s in range(SLOTS)] for q in range(ROWS)]

        def collect(d, e):
            owner = lax.rem(z + d, nz) * ny + lax.rem(y + e, ny)
            total = jnp.zeros((size, BLOCK), F32)
            for q in range(ROWS):
                for s in range(SLOTS):
                    total = total + jnp.where(named[q][s] == owner, 1.0, 0.0) * grecv[q, s, :size]
            return total

        others = sorted(range(1, ny), key=lambda e: -min(e, ny - e))
        for i, d in enumerate(beside_z):
            for e in range(ny):
                gacc[e, place[d], :size] = collect(d, e)
            sum_n(size, i).start()
        for g in far_rings:
            for e in others + [0]:
                for d in rings[g]:
                    gacc[e, place[d], :size] = collect(d, e)
                if e:
                    sum_y(size, g, e).start()

        def forward(g):
            for e in others:
                sum_y(size, g, e).wait_recv()
            for d in rings[g]:
                total = gacc[0, place[d], :size]
                for e in others:
                    total = total + gy[e, place[d], :size]
                if d:
                    gzs[d, :size] = total
                    sum_z(size, d).start()
            return total

        own = [collect(0, e) for e in range(ny)]
        for g in far_rings[:1]:
            forward(g)
        for i in range(len(beside_z)):
            sum_n(size, i).wait_recv()
            own = [own[e] + gn[i, e, :size] for e in range(ny)]
        for e in others + [0]:
            gacc[e, 0, :size] = own[e]
            if e:
                sum_y(size, 0, e).start()
        for g in far_rings[1:]:
            forward(g)
        total = forward(0)
        for d in far_first:
            sum_z(size, d).wait_recv()
            total = total + gz[d, :size]
        lgrad[mine(size), :] = total
        for k in ROW_ORDER:
            part_copy(size, k).start()
        part_out(size).start()

        for d in near_first:
            lib_z(size, d).wait_send()
        for g in range(len(rings)):
            for e in range(1, ny):
                lib_y(size, g, e).wait_send()
        for i in range(len(beside_z)):
            sum_n(size, i).wait_send()
        for d in far_first:
            sum_z(size, d).wait_send()
        for g in far_rings + [0]:
            for e in range(1, ny):
                sum_y(size, g, e).wait_send()
        for k in ROW_ORDER:
            spec_copy(size, k).wait_send()
            grad_copy(size, k).wait_send()

    for i in range(2):
        edge_rows(i, "send")
        edge_cols(i, "send")
    edge_corners("send")
    abund_out.wait()

    for p in range(ROWS):
        @pl.when(r != p)
        def _():
            part = pl.ds(start_of(p), SIZES[p % 2])
            far(lgrad.at[part], lgrad_hbm.at[part], send_c.at[0], recv_c.at[p], (r, c)).wait_recv()

    @by_core
    def _(size):
        part_out(size).wait()
        for k in ROW_ORDER:
            part_copy(size, k).wait_send()


def finish(abund_in, lgrad_in, abund_out, lgrad_out, abund, lgrad, sems_in, sems_out):
    rows = abund_in.shape[0] // COPIES
    ways = [(lgrad_in, lgrad, lgrad_out)]
    for i in range(COPIES):
        part = pl.ds(i * rows, rows)
        ways.append((abund_in.at[part], abund.at[part], abund_out.at[part]))
    reads = [pltpu.make_async_copy(way[0], way[1], sems_in.at[i]) for i, way in enumerate(ways)]
    writes = [pltpu.make_async_copy(way[1], way[2], sems_out.at[i]) for i, way in enumerate(ways)]
    for read in reads:
        read.start()
    for read, write in zip(reads, writes):
        read.wait()
        write.start()
    for write in writes:
        write.wait()


def local(cols, pixels, library, block_ids, counts):
    dma = pltpu.SemaphoreType.DMA
    ny = YS
    nz = cols // ny
    hbm = pl.BlockSpec(memory_space=pltpu.HBM)
    shapes = (
        jax.ShapeDtypeStruct((WIDE * TILE_H, TILE_W), F32),
        jax.ShapeDtypeStruct((BANDS, BLOCK), F32),
    )
    abundance, grad = pl.pallas_call(
        functools.partial(kernel, cols),
        out_shape=shapes,
        in_specs=[hbm] * 4,
        out_specs=(hbm, hbm),
        scratch_shapes=[
            pltpu.VMEM((BANDS * TILE_H, TILE_W), F32),
            pltpu.SMEM((ROWS, SLOTS, cols), jnp.int32),
            pltpu.SMEM((ROWS, cols), jnp.int32),
            pltpu.VMEM((WIDE + BANDS, PIX), BF16),
            pltpu.VMEM((WIDE + BANDS, PIX), BF16),
            pltpu.VMEM((ny, nz, PART, BLOCK), F32),
            pltpu.VMEM((ROWS, SLOTS, PART, BLOCK), F32),
            pltpu.VMEM((SLOTS, BANDS, BLOCK), F32),
            pltpu.VMEM((WIDE, PIX), F32),
            pltpu.VMEM((WIDE, PIX), F32),
            pltpu.VMEM((WIDE, PIX), F32),
            pltpu.VMEM((64, PIX), BF16),
            pltpu.VMEM((2, 2, WIDE, TILE_W), F32),
            pltpu.VMEM((2, 2, WIDE, TILE_W), F32),
            pltpu.VMEM((2, 32, WIDE), F32),
            pltpu.VMEM((2, 32, WIDE), F32),
            pltpu.VMEM((4, 8, WIDE), F32),
            pltpu.VMEM((4, 8, WIDE), F32),
            pltpu.VMEM((SLOTS, BANDS, BLOCK), F32),
            pltpu.VMEM((ROWS, SLOTS, PART, BLOCK), F32),
            pltpu.VMEM((ny, nz, PART, BLOCK), F32),
            pltpu.VMEM((2, ny, PART, BLOCK), F32),
            pltpu.VMEM((ny, nz, PART, BLOCK), F32),
            pltpu.VMEM((nz, PART, BLOCK), F32),
            pltpu.VMEM((nz, PART, BLOCK), F32),
            pltpu.VMEM((WIDE * TILE_H, TILE_W), F32),
            pltpu.VMEM((BANDS, BLOCK), F32),
            dma((nz,)), dma((nz,)),
            dma((nz, ny)), dma((nz, ny)),
            dma((ROWS,)), dma((ROWS,)),
            dma((2, 4)), dma((2, 4)),
            dma((4,)), dma((4,)),
            dma((ROWS,)), dma((ROWS,)),
            dma((2,)), dma((2,)),
            dma((nz, ny)), dma((nz, ny)),
            dma((nz,)), dma((nz,)),
            dma((ROWS,)), dma((ROWS,)),
            dma((4,)), dma((2,)),
        ],
        compiler_params=pltpu.CompilerParams(
            collective_id=0, has_side_effects=True, vmem_limit_bytes=VMEM_LIMIT
        ),
    )(
        pixels.reshape(BANDS * TILE_H, TILE_W), library,
        block_ids.transpose(0, 2, 1), counts,
    )
    abundance, grad = pl.pallas_call(
        finish,
        out_shape=shapes,
        in_specs=[hbm, hbm],
        out_specs=(hbm, hbm),
        scratch_shapes=[
            pltpu.VMEM((WIDE * TILE_H, TILE_W), F32),
            pltpu.VMEM((BANDS, BLOCK), F32),
            dma((COPIES + 1,)), dma((COPIES + 1,)),
        ],
        compiler_params=pltpu.CompilerParams(vmem_limit_bytes=VMEM_LIMIT),
    )(abundance, grad)
    return abundance.reshape(SLOTS, BLOCK, TILE_H, TILE_W), grad.T


def solution(mesh):
    placed = (P(None, "row", "col"), P(None, "col"), P(), P())
    return jax.shard_map(
        functools.partial(local, mesh.shape["col"]),
        mesh=mesh,
        in_specs=placed,
        out_specs=(P(None, None, "row", "col"), P("col", None)),
        check_vma=False,
    )
```
